512 devices in a mesh: row: 128 (over z_hi, y, x, core), col: 4 (over z_lo).
Axes of the slice: x: 4, y: 8, z: 8 (z_hi: 2, z_lo: 4; z = z_hi * 4 + z_lo), core: 2. Of those that a mesh axis runs over, the one named last changes fastest.
Arguments:
- coeffs: float32 [32, 512, 512], P('col', 'row'), may hold values from -0.01171875 to 0.01171875
- constraint_coeffs: float32 [2, 32], replicated, may hold values from 0.3 to 1
- alpha: float32 [1], replicated, may hold values from 0.95 to 1.05
- coset_shift: float32 [1], replicated, may hold values from 0.2 to 0.8
Outputs:
- evaluations: float32 [2, 32, 2048, 512], P(None, 'col', 'row')
- quotient: float32 [2, 2048, 512], P(None, 'row', 'col')
The draws below stay inside these ranges and needn't reach their ends.
All inputs are finite; a program needn't handle non-finite values.
Results may differ from the reference program's by a relative error of at most 0.000082.
Values sent between devices are 32-bit elements; how exact they have to be, the bound alone decides.
A program may use at most 64 MiB of HBM per device.

```python
import math
import jax
import jax.numpy as jnp

C = 32
BLOWUP = 4
INNER = 2048
LDE_ROWS = 1048576
TRACE_ROWS = 262144
OUTER = 512


def block_levels(stream_key, dims, pieces, smallest, largest):
    level, own = 1.0, jax.random.fold_in(stream_key, 6)
    for axis_at, parts in pieces:
        steps = jnp.exp(jax.random.uniform(jax.random.fold_in(own, axis_at), (parts,), jnp.float32, smallest / len(pieces), largest / len(pieces)))
        level = level * jnp.repeat(steps, dims[axis_at] // parts).reshape([-1 if axis == axis_at else 1 for axis in range(len(dims))])
    return level


def centred(stream_key, extent, scale, limit, split=(), kind=jnp.bfloat16):
    factor_of = block_levels(stream_key, extent, split, -0.22, 0.18) if split else 1.0
    array = jax.random.normal(stream_key, extent, jnp.float32) * scale * factor_of
    return jnp.minimum(jnp.maximum(array, -limit), limit).astype(kind)


def setup_inputs(seed: int = 0) -> dict:
    arg_keys = jax.random.split(jax.random.key(seed), 5)
    coeffs = centred(arg_keys[0], (C, OUTER, INNER // BLOWUP), TRACE_ROWS ** -0.5, 0.01171875, ((0, 4), (1, 128)), jnp.float32)
    constraint_coeffs = jnp.clip(jax.random.uniform(arg_keys[1], (2, C), jnp.float32, 0.3, 1.0), 0.3, 1.0)
    alpha = jnp.clip(jax.random.uniform(arg_keys[2], (1,), jnp.float32, 0.95, 1.05), 0.95, 1.05)
    coset_shift = jnp.clip(jax.random.uniform(arg_keys[3], (1,), jnp.float32, 0.2, 0.8), 0.2, 0.8)
    return {"coeffs": coeffs, "constraint_coeffs": constraint_coeffs, "alpha": alpha, "coset_shift": coset_shift}


def reference(coeffs, constraint_coeffs, alpha, coset_shift):
    coef = jnp.transpose(coeffs, (0, 2, 1)).reshape(C, TRACE_ROWS)
    shift = coset_shift[0]
    index = jnp.arange(TRACE_ROWS, dtype=jnp.int32)
    phase = index.astype(jnp.float32) * (shift * (2.0 * math.pi / LDE_ROWS))
    spectrum = coef * jnp.cos(phase) + 1j * (coef * jnp.sin(phase))
    spectrum = jnp.pad(spectrum, ((0, 0), (0, LDE_ROWS - TRACE_ROWS)))
    values = jnp.fft.ifft(spectrum, axis=1) * LDE_ROWS
    following = jnp.roll(values, -BLOWUP, axis=1)
    quad = constraint_coeffs[0][:, None]
    linear = constraint_coeffs[1][:, None]
    weights = jnp.power(alpha[0], jnp.arange(C).astype(jnp.float32))[:, None]
    numer = jnp.sum(weights * (following - quad * values * values - linear * values), axis=0)
    points = jnp.arange(LDE_ROWS, dtype=jnp.int32)
    theta = (shift + (points % BLOWUP).astype(jnp.float32)) * (2.0 * math.pi / BLOWUP)
    vanish = (jnp.cos(theta) - 1.0) + 1j * jnp.sin(theta)
    quot = numer / vanish
    laid = jnp.transpose(values.reshape(C, OUTER, INNER), (0, 2, 1))
    qlaid = jnp.transpose(quot.reshape(OUTER, INNER), (1, 0))
    evaluations = jnp.stack((jnp.real(laid), jnp.imag(laid)))
    quotient = jnp.stack((jnp.real(qlaid), jnp.imag(qlaid)))
    return evaluations, quotient
```

```python
import math

import jax
import jax.numpy as jnp
import ml_dtypes
import numpy as np
from jax import lax
from jax.experimental import pallas as pl
from jax.experimental.pallas import tpu as pltpu
from jax.sharding import PartitionSpec as P

MESH = pl.DeviceIdType.MESH
TAU = 2.0 * math.pi

COLS = 8
GROUPS = 4
ROWS = 128
HALF = 64
TILES = 8
K2 = 512
POINTS = 512
BLOCK = 16
STEP = 4
PEERS = HALF - 1
BARRIER = PEERS + 1 + (GROUPS - 1) + GROUPS


def split_table(table):
    high = table.astype(np.float32).astype(ml_dtypes.bfloat16)
    low = (table - high.astype(np.float64)).astype(np.float32).astype(ml_dtypes.bfloat16)
    return high, low


def inner_table():
    k2 = np.arange(K2)[:, None]
    point = np.arange(1024)[None, :]
    angle = (k2 * point % 2048) * (TAU / 2048)
    cosine = np.cos(angle).reshape(K2, TILES, 128)
    sine = np.sin(angle).reshape(K2, TILES, 128)
    return split_table(np.concatenate((cosine, sine), axis=2).transpose(1, 0, 2))


def outer_table():
    device = np.arange(HALF)[:, None, None]
    half = np.arange(2)[None, :, None]
    low = np.arange(4)[None, None, :]
    k1 = (256 * half + 4 * device + low).reshape(POINTS, 1)
    angle = (k1 * np.arange(POINTS)[None, :] % POINTS) * (TAU / POINTS)
    return split_table(np.concatenate((np.cos(angle), np.sin(angle)), axis=1))


def split(values):
    high = values.astype(jnp.bfloat16)
    return high, (values - high.astype(jnp.float32)).astype(jnp.bfloat16)


def dot(left, right):
    return jnp.dot(left, right, preferred_element_type=jnp.float32)


def swap_groups(pieces):
    lane = lax.broadcasted_iota(jnp.int32, pieces[0].shape, pieces[0].ndim - 1)
    axis = pieces[0].ndim - 1
    pieces = list(pieces)
    for bit in (4, 2, 1):
        keep = (lane // (16 * bit)) % 2 == 0
        for first in range(8):
            if first & bit:
                continue
            a, b = pieces[first], pieces[first + bit]
            pieces[first] = jnp.where(keep, a, pltpu.roll(b, 16 * bit, axis))
            pieces[first + bit] = jnp.where(keep, pltpu.roll(a, 128 - 16 * bit, axis), b)
    return pieces


def kernel(
    coeffs,
    constraint,
    alpha,
    coset,
    in_high,
    in_low,
    out_high,
    out_low,
    evaluations,
    quotient,
    both,
    ih,
    il,
    oh,
    ol,
    x_high,
    x_low,
    twist,
    outgoing,
    incoming,
    values,
    part_out,
    part_in,
    edge_out,
    edge_in,
    table_sem,
    pair_sem,
    all_sem,
    part_sem,
    edge_sem,
    store_sem,
):
    row = lax.axis_index("row")
    col = lax.axis_index("col")
    half = row // HALF
    place = row % HALF
    tile = place // 8
    core = place % 2
    base = half * HALF
    previous = (row + ROWS - 1) % ROWS
    following = (row + 1) % ROWS
    partner = (row + HALF) % ROWS

    barrier = pltpu.get_barrier_semaphore()

    def greet(device):
        pl.semaphore_signal(barrier, inc=1, device_id=device, device_id_type=MESH)

    greet((partner, col))

    @pl.loop(1, HALF)
    def _(i):
        greet((base + (place + i) % HALF, col))

    for i in range(1, GROUPS):
        greet((row, (col + i) % GROUPS))
    for i in range(GROUPS):
        greet((following, i))

    loads = [
        pltpu.make_async_copy(source, target, table_sem.at[i])
        for i, (source, target) in enumerate(
            ((in_high, ih), (in_low, il), (out_high, oh), (out_low, ol))
        )
    ]
    for load in loads:
        load.start()

    shift = coset[0]
    both[half] = coeffs[...]
    k2 = lax.broadcasted_iota(jnp.int32, (1, K2), 1)
    phase = k2.astype(jnp.float32) * (shift * (TAU / 2048))
    sign = (1 - 2 * ((k2 % 2) * half)).astype(jnp.float32)
    phase_cos = jnp.cos(phase) * sign
    phase_sin = jnp.sin(phase) * sign

    sub = lax.broadcasted_iota(jnp.int32, (8, 1024), 0)
    k1 = 256 * (sub // 4) + 4 * place + sub % 4
    point = 1024 * half + lax.broadcasted_iota(jnp.int32, (8, 1024), 1)
    k1_f = k1.astype(jnp.float32)
    angle = ((k1 * point).astype(jnp.float32) + k1_f * shift) * (TAU / 1048576)
    twist_cos = jnp.cos(angle)
    twist_sin = jnp.sin(angle)
    for t in range(TILES):
        twist[t, 0] = twist_cos[:, 128 * t : 128 * t + 128]
        twist[t, 1] = twist_sin[:, 128 * t : 128 * t + 128]

    pl.semaphore_wait(barrier, BARRIER)

    pair = pltpu.make_async_remote_copy(
        src_ref=coeffs,
        dst_ref=both.at[half],
        send_sem=pair_sem.at[0],
        recv_sem=pair_sem.at[1],
        device_id=(partner, col),
        device_id_type=MESH,
    )
    pair.start()
    pair.wait()

    x = jnp.concatenate((both[0], both[1]), axis=1).reshape(64, K2)
    x = jnp.concatenate((x * phase_cos, x * phase_sin), axis=0)
    high, low = split(x)
    x_high[...] = high
    x_low[...] = low
    loads[0].wait()
    loads[1].wait()

    def send(device):
        return pltpu.make_async_remote_copy(
            src_ref=outgoing.at[device],
            dst_ref=incoming.at[place],
            send_sem=all_sem.at[0],
            recv_sem=all_sem.at[1],
            device_id=(base + device, col),
            device_id_type=MESH,
        )

    @pl.loop(0, TILES)
    def _(i):
        offset = (i + 1) // 2 * (2 * ((i + 1) % 2) - 1)
        t = (tile + 4 + offset * (1 - 2 * core) + 8) % TILES
        ah, al = x_high[...], x_low[...]
        bh, bl = ih[t], il[t]
        y = dot(ah, bh) + (dot(al, bh) + dot(ah, bl))
        real = (y[:64, :128] - y[64:, 128:]).reshape(COLS, 8, 128)
        imag = (y[:64, 128:] + y[64:, :128]).reshape(COLS, 8, 128)
        cosine, sine = twist[t, 0][None], twist[t, 1][None]
        turned_real = real * cosine - imag * sine
        turned_imag = real * sine + imag * cosine
        swapped_real = swap_groups([turned_real[c] for c in range(COLS)])
        swapped_imag = swap_groups([turned_imag[c] for c in range(COLS)])
        for d in range(8):
            outgoing[8 * t + d, :, :128] = swapped_real[d]
            outgoing[8 * t + d, :, 128:] = swapped_imag[d]

        @pl.loop(0, 8)
        def _(j):
            device = 8 * t + (place + j) % 8

            @pl.when(device != place)
            def _():
                send(device).start()

    incoming[place] = outgoing[place]
    everything = pltpu.make_async_remote_copy(
        src_ref=outgoing.at[pl.ds(0, PEERS)],
        dst_ref=incoming.at[pl.ds(0, PEERS)],
        send_sem=all_sem.at[0],
        recv_sem=all_sem.at[1],
        device_id=(partner, col),
        device_id_type=MESH,
    )
    loads[2].wait()
    loads[3].wait()
    everything.wait_recv()

    held = incoming[...].reshape(POINTS, 256).T
    rh, rl = split(held)
    th, tl = oh[...], ol[...]
    v = dot(rh, th) + (dot(rl, th) + dot(rh, tl))
    real = (v[:128, :POINTS] - v[128:, POINTS:]).reshape(COLS, BLOCK, POINTS)
    imag = (v[:128, POINTS:] + v[128:, :POINTS]).reshape(COLS, BLOCK, POINTS)
    values[0] = real
    values[1] = imag
    store = pltpu.make_async_copy(values, evaluations, store_sem)
    store.start()

    a1 = alpha[0]
    a2 = a1 * a1
    a4 = a2 * a2
    a8 = a4 * a4
    weight = jnp.where(col % 2 == 1, a8, 1.0) * jnp.where(col // 2 == 1, a8 * a8, 1.0)
    ahead_real = ahead_imag = sum_real = sum_imag = 0.0
    for c in range(COLS):
        quad = constraint[0, COLS * col + c]
        linear = constraint[1, COLS * col + c]
        vr, vi = real[c], imag[c]
        ahead_real += weight * vr
        ahead_imag += weight * vi
        sum_real += weight * (quad * (vr * vr - vi * vi) + linear * vr)
        sum_imag += weight * (quad * (2.0 * vr * vi) + linear * vi)
        weight = weight * a1

    none = jnp.zeros((STEP, POINTS), jnp.float32)
    sum_real = jnp.concatenate((ahead_real[STEP:], none), axis=0) - sum_real
    sum_imag = jnp.concatenate((ahead_imag[STEP:], none), axis=0) - sum_imag
    edge = jnp.concatenate((ahead_real[:STEP], ahead_imag[:STEP]), axis=0)
    edge = jnp.where(row == 0, pltpu.roll(edge, POINTS - 1, 1), edge)
    for q in range(GROUPS):
        edge_out[q] = edge[:, 128 * q : 128 * q + 128]
        part_out[q, 0] = sum_real[:, 128 * q : 128 * q + 128]
        part_out[q, 1] = sum_imag[:, 128 * q : 128 * q + 128]

    def send_part(target):
        return pltpu.make_async_remote_copy(
            src_ref=part_out.at[target],
            dst_ref=part_in.at[col],
            send_sem=part_sem.at[0],
            recv_sem=part_sem.at[1],
            device_id=(row, target),
            device_id_type=MESH,
        )

    for i in range(1, GROUPS):
        send_part((col + i) % GROUPS).start()
    for q in range(GROUPS):
        pltpu.make_async_remote_copy(
            src_ref=edge_out.at[q],
            dst_ref=edge_in.at[col],
            send_sem=edge_sem.at[0],
            recv_sem=edge_sem.at[1],
            device_id=(previous, q),
            device_id_type=MESH,
        ).start()
    part_in[col] = part_out[col]

    point = lax.broadcasted_iota(jnp.int32, (BLOCK, 128), 0) % STEP
    theta = (shift + point.astype(jnp.float32)) * (TAU / STEP)
    van_real = jnp.cos(theta) - 1.0
    van_imag = jnp.sin(theta)
    denominator = van_real * van_real + van_imag * van_imag

    parts = pltpu.make_async_remote_copy(
        src_ref=part_out.at[pl.ds(0, GROUPS - 1)],
        dst_ref=part_in.at[pl.ds(0, GROUPS - 1)],
        send_sem=part_sem.at[0],
        recv_sem=part_sem.at[1],
        device_id=(partner, col),
        device_id_type=MESH,
    )
    edges = pltpu.make_async_remote_copy(
        src_ref=edge_out,
        dst_ref=edge_in,
        send_sem=edge_sem.at[0],
        recv_sem=edge_sem.at[1],
        device_id=(partner, col),
        device_id_type=MESH,
    )
    parts.wait_recv()
    edges.wait_recv()
    part = (part_in[0] + part_in[1]) + (part_in[2] + part_in[3])
    edge = (edge_in[0] + edge_in[1]) + (edge_in[2] + edge_in[3])
    none = jnp.zeros((BLOCK - STEP, 128), jnp.float32)
    num_real = part[0] + jnp.concatenate((none, edge[:STEP]), axis=0)
    num_imag = part[1] + jnp.concatenate((none, edge[STEP:]), axis=0)
    quotient[0] = (num_real * van_real + num_imag * van_imag) / denominator
    quotient[1] = (num_imag * van_real - num_real * van_imag) / denominator

    everything.wait_send()
    parts.wait_send()
    edges.wait_send()
    store.wait()


def per_device(coeffs, constraint_coeffs, alpha, coset_shift):
    tables = inner_table() + outer_table()
    any_space = pl.BlockSpec(memory_space=pl.ANY)
    vmem = pl.BlockSpec(memory_space=pltpu.VMEM)
    smem = pl.BlockSpec(memory_space=pltpu.SMEM)
    f32 = jnp.float32
    bf16 = jnp.bfloat16
    return pl.pallas_call(
        kernel,
        out_shape=(
            jax.ShapeDtypeStruct((2, COLS, BLOCK, POINTS), f32),
            jax.ShapeDtypeStruct((2, BLOCK, 128), f32),
        ),
        in_specs=[vmem, smem, smem, smem] + [any_space] * 4,
        out_specs=(any_space, vmem),
        scratch_shapes=[
            pltpu.VMEM((2, COLS, 4, K2), f32),
            pltpu.VMEM((TILES, K2, 256), bf16),
            pltpu.VMEM((TILES, K2, 256), bf16),
            pltpu.VMEM((POINTS, 2 * POINTS), bf16),
            pltpu.VMEM((POINTS, 2 * POINTS), bf16),
            pltpu.VMEM((128, K2), bf16),
            pltpu.VMEM((128, K2), bf16),
            pltpu.VMEM((TILES, 2, 8, 128), f32),
            pltpu.VMEM((HALF, 8, 256), f32),
            pltpu.VMEM((HALF, 8, 256), f32),
            pltpu.VMEM((2, COLS, BLOCK, POINTS), f32),
            pltpu.VMEM((GROUPS, 2, BLOCK, 128), f32),
            pltpu.VMEM((GROUPS, 2, BLOCK, 128), f32),
            pltpu.VMEM((GROUPS, 8, 128), f32),
            pltpu.VMEM((GROUPS, 8, 128), f32),
            pltpu.SemaphoreType.DMA((4,)),
            pltpu.SemaphoreType.DMA((2,)),
            pltpu.SemaphoreType.DMA((2,)),
            pltpu.SemaphoreType.DMA((2,)),
            pltpu.SemaphoreType.DMA((2,)),
            pltpu.SemaphoreType.DMA,
        ],
        compiler_params=pltpu.CompilerParams(
            collective_id=0, has_side_effects=True, vmem_limit_bytes=48 * 1024 * 1024
        ),
    )(coeffs, constraint_coeffs, alpha, coset_shift, *tables)


def solution(mesh):
    in_specs = (P("col", "row", None), P(), P(), P())
    out_specs = (P(None, "col", "row", None), P(None, "row", "col"))
    return jax.shard_map(
        per_device, mesh=mesh, in_specs=in_specs, out_specs=out_specs, check_vma=False
    )
```

```python
import math

import jax
import jax.numpy as jnp
import ml_dtypes
import numpy as np
from jax import lax
from jax.experimental import pallas as pl
from jax.experimental.pallas import tpu as pltpu
from jax.sharding import PartitionSpec as P

MESH = pl.DeviceIdType.MESH
TAU = 2.0 * math.pi

COLS = 8
GROUPS = 4
ROWS = 128
HALF = 64
TILES = 8
K2 = 512
POINTS = 512
BLOCK = 16
STEP = 4
PEERS = HALF - 1
BARRIER = PEERS + 1 + (GROUPS - 1) + GROUPS


def split_table(table):
    high = table.astype(np.float32).astype(ml_dtypes.bfloat16)
    low = (table - high.astype(np.float64)).astype(np.float32).astype(ml_dtypes.bfloat16)
    return high, low


def inner_table():
    k2 = np.arange(K2)[:, None]
    point = np.arange(1024)[None, :]
    angle = (k2 * point % 2048) * (TAU / 2048)
    cosine = np.cos(angle).reshape(K2, TILES, 128)
    sine = np.sin(angle).reshape(K2, TILES, 128)
    table = np.concatenate((cosine, sine), axis=2).transpose(1, 0, 2)
    return np.stack(split_table(table), axis=1)


def outer_table():
    place = np.arange(HALF)[:, None]
    low = np.arange(4)[None, :]
    k1 = np.stack([256 * part + 4 * place + low for part in range(2)])
    angle = (k1[..., None] * np.arange(POINTS) % POINTS) * (TAU / POINTS)
    cosine, sine = np.cos(angle), np.sin(angle)
    from_real = np.concatenate((cosine, sine), axis=3)
    from_imag = np.concatenate((-sine, cosine), axis=3)
    table = np.stack((from_real, from_imag), axis=2).reshape(2, 2 * 256, 2 * POINTS)
    return np.stack(split_table(table), axis=1)


def split(values):
    high = values.astype(jnp.bfloat16)
    return high, (values - high.astype(jnp.float32)).astype(jnp.bfloat16)


def dot(left, right):
    return jnp.dot(left, right, preferred_element_type=jnp.float32)


def swap_groups(pieces):
    lane = lax.broadcasted_iota(jnp.int32, pieces[0].shape, pieces[0].ndim - 1)
    axis = pieces[0].ndim - 1
    pieces = list(pieces)
    for bit in (4, 2, 1):
        keep = (lane // (16 * bit)) % 2 == 0
        for first in range(8):
            if first & bit:
                continue
            a, b = pieces[first], pieces[first + bit]
            pieces[first] = jnp.where(keep, a, pltpu.roll(b, 16 * bit, axis))
            pieces[first + bit] = jnp.where(keep, pltpu.roll(a, 128 - 16 * bit, axis), b)
    return pieces


def kernel(
    coeffs,
    constraint,
    alpha,
    coset,
    inner_hbm,
    outer_hbm,
    evaluations,
    quotient,
    own,
    other,
    inner,
    outer,
    x_split,
    twist,
    outgoing,
    incoming,
    part_out,
    part_in,
    edge_out,
    edge_in,
    table_sem,
    own_sem,
    pair_sem,
    send_sem,
    recv_sem,
    part_sem,
    edge_sem,
):
    row = lax.axis_index("row")
    col = lax.axis_index("col")
    half = row // HALF
    place = row % HALF
    tile = place // 8
    core = place % 2
    base = half * HALF
    previous = (row + ROWS - 1) % ROWS
    following = (row + 1) % ROWS
    partner = (row + HALF) % ROWS

    barrier = pltpu.get_barrier_semaphore()

    def greet(device):
        pl.semaphore_signal(barrier, inc=1, device_id=device, device_id_type=MESH)

    greet((partner, col))

    @pl.loop(1, HALF)
    def _(i):
        greet((base + (place + i) % HALF, col))

    for i in range(1, GROUPS):
        greet((row, (col + i) % GROUPS))
    for i in range(GROUPS):
        greet((following, i))

    def tile_of(i):
        offset = (i + 1) // 2 * (2 * ((i + 1) % 2) - 1)
        return (tile + 4 + offset * (1 - 2 * core) + 8) % TILES

    def load_tile(t):
        return pltpu.make_async_copy(inner_hbm.at[t], inner.at[t], table_sem.at[t])

    load_own = pltpu.make_async_copy(coeffs, own, own_sem)
    load_own.start()

    @pl.loop(0, TILES)
    def _(i):
        load_tile(tile_of(i)).start()

    load_outer = pltpu.make_async_copy(outer_hbm, outer, table_sem.at[TILES])
    load_outer.start()

    shift = coset[0]
    k2 = lax.broadcasted_iota(jnp.int32, (1, K2), 1)
    phase = k2.astype(jnp.float32) * (shift * (TAU / 2048))
    sign = (1 - 2 * ((k2 % 2) * half)).astype(jnp.float32)
    phase_cos = jnp.cos(phase) * sign
    phase_sin = jnp.sin(phase) * sign

    sub = lax.broadcasted_iota(jnp.int32, (8, 1024), 0)
    k1 = 256 * ((half + sub // 4) % 2) + 4 * place + sub % 4
    point = 1024 * half + lax.broadcasted_iota(jnp.int32, (8, 1024), 1)
    k1_f = k1.astype(jnp.float32)
    angle = ((k1 * point).astype(jnp.float32) + k1_f * shift) * (TAU / 1048576)
    cosine, sine = jnp.cos(angle), jnp.sin(angle)
    cosine_turned, sine_turned = pltpu.roll(cosine, 4, 0), pltpu.roll(sine, 4, 0)
    upper = sub < 4
    pairs = (
        (jnp.where(upper, cosine, cosine_turned), jnp.where(upper, -sine, sine_turned)),
        (jnp.where(upper, cosine_turned, cosine), jnp.where(upper, -sine_turned, sine)),
    )
    for p in range(2):
        for t in range(TILES):
            twist[p, t, 0] = pairs[p][0][:, 128 * t : 128 * t + 128]
            twist[p, t, 1] = pairs[p][1][:, 128 * t : 128 * t + 128]

    def prepare(p, source):
        x = source[...]
        x = jnp.concatenate((x * phase_cos, x * phase_sin), axis=1).reshape(64, K2)
        high, low = split(x)
        x_split[p, 0] = high
        x_split[p, 1] = low

    load_own.wait()
    prepare(0, own)
    pl.semaphore_wait(barrier, BARRIER)

    pair = pltpu.make_async_remote_copy(
        src_ref=coeffs,
        dst_ref=other,
        send_sem=pair_sem.at[0],
        recv_sem=pair_sem.at[1],
        device_id=(partner, col),
        device_id_type=MESH,
    )
    pair.start()

    def send(p, device):
        return pltpu.make_async_remote_copy(
            src_ref=outgoing.at[p, device],
            dst_ref=incoming.at[(half + p) % 2, place],
            send_sem=send_sem.at[p],
            recv_sem=recv_sem.at[p],
            device_id=(base + device, col),
            device_id_type=MESH,
        )

    def whole(p):
        return pltpu.make_async_remote_copy(
            src_ref=outgoing.at[p, pl.ds(0, PEERS)],
            dst_ref=incoming.at[(half + p) % 2, pl.ds(0, PEERS)],
            send_sem=send_sem.at[p],
            recv_sem=recv_sem.at[p],
            device_id=(partner, col),
            device_id_type=MESH,
        )

    minus = jnp.where(lax.broadcasted_iota(jnp.int32, (1, 8, 128), 1) < 4, -1.0, 1.0)

    def run_tile(p, t):
        ah, al = x_split[p, 0], x_split[p, 1]
        bh, bl = inner[t, 0], inner[t, 1]
        y = dot(ah, bh) + (dot(al, bh) + dot(ah, bl))
        z = y[:, :128].reshape(COLS, 8, 128)
        z = z + minus * pltpu.roll(y[:, 128:].reshape(COLS, 8, 128), 4, 1)
        z = z * twist[p, t, 0][None] + pltpu.roll(z, 4, 1) * twist[p, t, 1][None]
        swapped = swap_groups([z[c] for c in range(COLS)])
        for d in range(8):
            outgoing[p, 8 * t + d] = swapped[d]

    def send_tile(p, t):
        @pl.loop(0, 8)
        def _(j):
            device = 8 * t + (place + j) % 8

            @pl.when(device != place)
            def _():
                send(p, device).start()

    @pl.loop(0, TILES)
    def _(i):
        t = tile_of(i)
        load_tile(t).wait()
        run_tile(0, t)
        send_tile(0, t)

    incoming[half, place] = outgoing[0, place]
    pair.wait_recv()
    prepare(1, other)

    @pl.loop(0, TILES)
    def _(i):
        t = tile_of(i)
        run_tile(1, t)
        send_tile(1, t)

    incoming[1 - half, place] = outgoing[1, place]
    load_outer.wait()

    def finish(p):
        whole(p).wait_recv()
        part = (half + p) % 2
        held = incoming[part].reshape(POINTS, 128).T
        rh, rl = split(held)
        th, tl = outer[part, 0], outer[part, 1]
        return dot(rh, th) + (dot(rl, th) + dot(rh, tl))

    v = finish(0)
    v = v + finish(1)
    real = v[:, :POINTS].reshape(COLS, BLOCK, POINTS)
    imag = v[:, POINTS:].reshape(COLS, BLOCK, POINTS)
    evaluations[0] = real
    evaluations[1] = imag

    a1 = alpha[0]
    a2 = a1 * a1
    a4 = a2 * a2
    a8 = a4 * a4
    weight = jnp.where(col % 2 == 1, a8, 1.0) * jnp.where(col // 2 == 1, a8 * a8, 1.0)
    ahead_real = ahead_imag = sum_real = sum_imag = 0.0
    for c in range(COLS):
        quad = constraint[0, COLS * col + c]
        linear = constraint[1, COLS * col + c]
        vr, vi = real[c], imag[c]
        ahead_real += weight * vr
        ahead_imag += weight * vi
        sum_real += weight * (quad * (vr * vr - vi * vi) + linear * vr)
        sum_imag += weight * (quad * (2.0 * vr * vi) + linear * vi)
        weight = weight * a1

    none = jnp.zeros((STEP, POINTS), jnp.float32)
    sum_real = jnp.concatenate((ahead_real[STEP:], none), axis=0) - sum_real
    sum_imag = jnp.concatenate((ahead_imag[STEP:], none), axis=0) - sum_imag
    edge = jnp.concatenate((ahead_real[:STEP], ahead_imag[:STEP]), axis=0)
    edge = jnp.where(row == 0, pltpu.roll(edge, POINTS - 1, 1), edge)
    for q in range(GROUPS):
        edge_out[q] = edge[:, 128 * q : 128 * q + 128]
        part_out[q, 0] = sum_real[:, 128 * q : 128 * q + 128]
        part_out[q, 1] = sum_imag[:, 128 * q : 128 * q + 128]

    def send_part(target):
        return pltpu.make_async_remote_copy(
            src_ref=part_out.at[target],
            dst_ref=part_in.at[col],
            send_sem=part_sem.at[0],
            recv_sem=part_sem.at[1],
            device_id=(row, target),
            device_id_type=MESH,
        )

    for i in range(1, GROUPS):
        send_part((col + i) % GROUPS).start()
    for q in range(GROUPS):
        pltpu.make_async_remote_copy(
            src_ref=edge_out.at[q],
            dst_ref=edge_in.at[col],
            send_sem=edge_sem.at[0],
            recv_sem=edge_sem.at[1],
            device_id=(previous, q),
            device_id_type=MESH,
        ).start()
    part_in[col] = part_out[col]

    point = lax.broadcasted_iota(jnp.int32, (BLOCK, 128), 0) % STEP
    theta = (shift + point.astype(jnp.float32)) * (TAU / STEP)
    van_real = jnp.cos(theta) - 1.0
    van_imag = jnp.sin(theta)
    denominator = van_real * van_real + van_imag * van_imag

    parts = pltpu.make_async_remote_copy(
        src_ref=part_out.at[pl.ds(0, GROUPS - 1)],
        dst_ref=part_in.at[pl.ds(0, GROUPS - 1)],
        send_sem=part_sem.at[0],
        recv_sem=part_sem.at[1],
        device_id=(partner, col),
        device_id_type=MESH,
    )
    edges = pltpu.make_async_remote_copy(
        src_ref=edge_out,
        dst_ref=edge_in,
        send_sem=edge_sem.at[0],
        recv_sem=edge_sem.at[1],
        device_id=(partner, col),
        device_id_type=MESH,
    )
    parts.wait_recv()
    edges.wait_recv()
    part = (part_in[0] + part_in[1]) + (part_in[2] + part_in[3])
    edge = (edge_in[0] + edge_in[1]) + (edge_in[2] + edge_in[3])
    none = jnp.zeros((BLOCK - STEP, 128), jnp.float32)
    num_real = part[0] + jnp.concatenate((none, edge[:STEP]), axis=0)
    num_imag = part[1] + jnp.concatenate((none, edge[STEP:]), axis=0)
    quotient[0] = (num_real * van_real + num_imag * van_imag) / denominator
    quotient[1] = (num_imag * van_real - num_real * van_imag) / denominator

    pair.wait_send()
    whole(0).wait_send()
    whole(1).wait_send()
    parts.wait_send()
    edges.wait_send()


def per_device(coeffs, constraint_coeffs, alpha, coset_shift):
    tables = inner_table(), outer_table()
    hbm = pl.BlockSpec(memory_space=pltpu.HBM)
    vmem = pl.BlockSpec(memory_space=pltpu.VMEM)
    smem = pl.BlockSpec(memory_space=pltpu.SMEM)
    f32 = jnp.float32
    bf16 = jnp.bfloat16
    return pl.pallas_call(
        kernel,
        out_shape=(
            jax.ShapeDtypeStruct((2, COLS, BLOCK, POINTS), f32),
            jax.ShapeDtypeStruct((2, BLOCK, 128), f32),
        ),
        in_specs=[hbm, smem, smem, smem] + [hbm] * 2,
        out_specs=(vmem, vmem),
        scratch_shapes=[
            pltpu.VMEM((COLS, 4, K2), f32),
            pltpu.VMEM((COLS, 4, K2), f32),
            pltpu.VMEM((TILES, 2, K2, 256), bf16),
            pltpu.VMEM((2, 2, POINTS, 2 * POINTS), bf16),
            pltpu.VMEM((2, 2, 64, K2), bf16),
            pltpu.VMEM((2, TILES, 2, 8, 128), f32),
            pltpu.VMEM((2, HALF, 8, 128), f32),
            pltpu.VMEM((2, HALF, 8, 128), f32),
            pltpu.VMEM((GROUPS, 2, BLOCK, 128), f32),
            pltpu.VMEM((GROUPS, 2, BLOCK, 128), f32),
            pltpu.VMEM((GROUPS, 8, 128), f32),
            pltpu.VMEM((GROUPS, 8, 128), f32),
            pltpu.SemaphoreType.DMA((TILES + 1,)),
            pltpu.SemaphoreType.DMA,
            pltpu.SemaphoreType.DMA((2,)),
            pltpu.SemaphoreType.DMA((2,)),
            pltpu.SemaphoreType.DMA((2,)),
            pltpu.SemaphoreType.DMA((2,)),
            pltpu.SemaphoreType.DMA((2,)),
        ],
        compiler_params=pltpu.CompilerParams(
            collective_id=0, has_side_effects=True, vmem_limit_bytes=62 * 1024 * 1024
        ),
    )(coeffs, constraint_coeffs, alpha, coset_shift, *tables)


def solution(mesh):
    in_specs = (P("col", "row", None), P(), P(), P())
    out_specs = (P(None, "col", "row", None), P(None, "row", "col"))
    return jax.shard_map(
        per_device, mesh=mesh, in_specs=in_specs, out_specs=out_specs, check_vma=False
    )
```

```python
import math

import jax
import jax.numpy as jnp
import ml_dtypes
import numpy as np
from jax import lax
from jax.experimental import pallas as pl
from jax.experimental.pallas import tpu as pltpu
from jax.sharding import PartitionSpec as P

MESH = pl.DeviceIdType.MESH
TAU = 2.0 * math.pi

COLS = 8
GROUPS = 4
ROWS = 128
HALF = 64
TILES = 8
K2 = 512
POINTS = 512
BLOCK = 16
STEP = 4
PEERS = HALF - 1
BARRIER = PEERS + 1 + (GROUPS - 1) + GROUPS


def split_table(table):
    high = table.astype(np.float32).astype(ml_dtypes.bfloat16)
    low = (table - high.astype(np.float64)).astype(np.float32).astype(ml_dtypes.bfloat16)
    return high, low


def inner_table():
    k2 = np.arange(K2)[:, None]
    point = np.arange(1024)[None, :]
    angle = (k2 * point % 2048) * (TAU / 2048)
    cosine = np.cos(angle).reshape(K2, TILES, 128)
    sine = np.sin(angle).reshape(K2, TILES, 128)
    table = np.concatenate((cosine, sine), axis=2).transpose(1, 0, 2)
    return np.stack(split_table(table), axis=1)


def outer_table():
    place = np.arange(HALF)[:, None]
    low = np.arange(4)[None, :]
    k1 = np.stack([256 * part + 4 * place + low for part in range(2)])
    angle = (k1[..., None] * np.arange(POINTS) % POINTS) * (TAU / POINTS)
    cosine, sine = np.cos(angle), np.sin(angle)
    from_real = np.concatenate((cosine, sine), axis=3)
    from_imag = np.concatenate((-sine, cosine), axis=3)
    table = np.stack((from_real, from_imag), axis=2).reshape(2, 2 * 256, 2 * POINTS)
    return np.stack(split_table(table), axis=1)


def split(values):
    high = values.astype(jnp.bfloat16)
    return high, (values - high.astype(jnp.float32)).astype(jnp.bfloat16)


def dot(left, right):
    return jnp.dot(left, right, preferred_element_type=jnp.float32)


def swap_groups(pieces):
    lane = lax.broadcasted_iota(jnp.int32, pieces[0].shape, pieces[0].ndim - 1)
    axis = pieces[0].ndim - 1
    pieces = list(pieces)
    for bit in (4, 2, 1):
        keep = (lane // (16 * bit)) % 2 == 0
        for first in range(8):
            if first & bit:
                continue
            a, b = pieces[first], pieces[first + bit]
            pieces[first] = jnp.where(keep, a, pltpu.roll(b, 16 * bit, axis))
            pieces[first + bit] = jnp.where(keep, pltpu.roll(a, 128 - 16 * bit, axis), b)
    return pieces


def kernel(
    coeffs,
    constraint_hbm,
    alpha,
    coset,
    inner_hbm,
    outer_hbm,
    evaluations,
    quotient,
    own,
    other,
    inner,
    outer,
    x_split,
    twist,
    outgoing,
    incoming,
    part_out,
    part_in,
    edge_out,
    edge_in,
    table_sem,
    own_sem,
    pair_sem,
    send_sem,
    recv_sem,
    part_sem,
    edge_sem,
    constraint,
    small_sem,
):
    row = lax.axis_index("row")
    col = lax.axis_index("col")
    half = row // HALF
    place = row % HALF
    tile = place // 8
    core = place % 2
    base = half * HALF
    previous = (row + ROWS - 1) % ROWS
    following = (row + 1) % ROWS
    partner = (row + HALF) % ROWS

    barrier = pltpu.get_barrier_semaphore()

    def greet(device):
        pl.semaphore_signal(barrier, inc=1, device_id=device, device_id_type=MESH)

    def tile_of(i):
        offset = (i + 1) // 2 * (2 * ((i + 1) % 2) - 1)
        return (tile + 4 + offset * (1 - 2 * core) + 8) % TILES

    def load_tile(t):
        return pltpu.make_async_copy(inner_hbm.at[t], inner.at[t], table_sem.at[t])

    load_own = pltpu.make_async_copy(coeffs, own, own_sem)
    load_own.start()
    load_small = pltpu.make_async_copy(constraint_hbm, constraint, small_sem)
    load_small.start()

    @pl.loop(0, TILES)
    def _(i):
        load_tile(tile_of(i)).start()

    load_outer = pltpu.make_async_copy(outer_hbm, outer, table_sem.at[TILES])
    load_outer.start()

    greet((partner, col))
    for i in range(1, HALF):
        greet((base + (place + i) % HALF, col))
    for i in range(1, GROUPS):
        greet((row, (col + i) % GROUPS))
    for i in range(GROUPS):
        greet((following, i))

    shift = coset[0]
    k2 = lax.broadcasted_iota(jnp.int32, (1, K2), 1)
    phase = k2.astype(jnp.float32) * (shift * (TAU / 2048))
    sign = (1 - 2 * ((k2 % 2) * half)).astype(jnp.float32)
    phase_cos = jnp.cos(phase) * sign
    phase_sin = jnp.sin(phase) * sign

    sub = lax.broadcasted_iota(jnp.int32, (8, 1024), 0)
    k1 = 256 * ((half + sub // 4) % 2) + 4 * place + sub % 4
    point = 1024 * half + lax.broadcasted_iota(jnp.int32, (8, 1024), 1)
    k1_f = k1.astype(jnp.float32)
    angle = ((k1 * point).astype(jnp.float32) + k1_f * shift) * (TAU / 1048576)
    cosine, sine = jnp.cos(angle), jnp.sin(angle)
    cosine_turned, sine_turned = pltpu.roll(cosine, 4, 0), pltpu.roll(sine, 4, 0)
    upper = sub < 4
    pairs = (
        (jnp.where(upper, cosine, cosine_turned), jnp.where(upper, -sine, sine_turned)),
        (jnp.where(upper, cosine_turned, cosine), jnp.where(upper, -sine_turned, sine)),
    )
    for p in range(2):
        for t in range(TILES):
            twist[p, t, 0] = pairs[p][0][:, 128 * t : 128 * t + 128]
            twist[p, t, 1] = pairs[p][1][:, 128 * t : 128 * t + 128]

    def prepare(p, source):
        x = source[...]
        x = jnp.concatenate((x * phase_cos, x * phase_sin), axis=1).reshape(64, K2)
        high, low = split(x)
        x_split[p, 0] = high
        x_split[p, 1] = low

    load_own.wait()
    prepare(0, own)
    pl.semaphore_wait(barrier, BARRIER)

    pair = pltpu.make_async_remote_copy(
        src_ref=coeffs,
        dst_ref=other,
        send_sem=pair_sem.at[0],
        recv_sem=pair_sem.at[1],
        device_id=(partner, col),
        device_id_type=MESH,
    )
    pair.start()

    def send(p, device):
        return pltpu.make_async_remote_copy(
            src_ref=outgoing.at[p, device],
            dst_ref=incoming.at[(half + p) % 2, place],
            send_sem=send_sem.at[p],
            recv_sem=recv_sem.at[p],
            device_id=(base + device, col),
            device_id_type=MESH,
        )

    def whole(p):
        return pltpu.make_async_remote_copy(
            src_ref=outgoing.at[p, pl.ds(0, PEERS)],
            dst_ref=incoming.at[(half + p) % 2, pl.ds(0, PEERS)],
            send_sem=send_sem.at[p],
            recv_sem=recv_sem.at[p],
            device_id=(partner, col),
            device_id_type=MESH,
        )

    minus = jnp.where(lax.broadcasted_iota(jnp.int32, (1, 8, 128), 1) < 4, -1.0, 1.0)

    def run_tile(p, t):
        ah, al = x_split[p, 0], x_split[p, 1]
        bh, bl = inner[t, 0], inner[t, 1]
        y = dot(ah, bh) + (dot(al, bh) + dot(ah, bl))
        z = y[:, :128].reshape(COLS, 8, 128)
        z = z + minus * pltpu.roll(y[:, 128:].reshape(COLS, 8, 128), 4, 1)
        z = z * twist[p, t, 0][None] + pltpu.roll(z, 4, 1) * twist[p, t, 1][None]
        swapped = swap_groups([z[c] for c in range(COLS)])
        for d in range(8):
            outgoing[p, 8 * t + d] = swapped[d]

    def send_tile(p, t, first):
        for j in range(first, 8):
            send(p, 8 * t + (place + j) % 8).start()

    @pl.loop(0, TILES - 1)
    def _(i):
        t = tile_of(i)
        load_tile(t).wait()
        run_tile(0, t)
        send_tile(0, t, 0)

    load_tile(tile).wait()
    run_tile(0, tile)
    send_tile(0, tile, 1)

    incoming[half, place] = outgoing[0, place]
    pair.wait_recv()
    prepare(1, other)

    @pl.loop(0, TILES - 1)
    def _(i):
        t = tile_of(i)
        run_tile(1, t)
        send_tile(1, t, 0)

    run_tile(1, tile)
    send_tile(1, tile, 1)

    incoming[1 - half, place] = outgoing[1, place]
    load_outer.wait()

    def finish(p):
        whole(p).wait_recv()
        part = (half + p) % 2
        held = incoming[part].reshape(POINTS, 128).T
        rh, rl = split(held)
        th, tl = outer[part, 0], outer[part, 1]
        return dot(rh, th) + (dot(rl, th) + dot(rh, tl))

    v = finish(0)
    v = v + finish(1)
    real = v[:, :POINTS].reshape(COLS, BLOCK, POINTS)
    imag = v[:, POINTS:].reshape(COLS, BLOCK, POINTS)
    evaluations[0] = real
    evaluations[1] = imag

    load_small.wait()
    a1 = alpha[0]
    a2 = a1 * a1
    a4 = a2 * a2
    a8 = a4 * a4
    weight = jnp.where(col % 2 == 1, a8, 1.0) * jnp.where(col // 2 == 1, a8 * a8, 1.0)
    ahead_real = ahead_imag = sum_real = sum_imag = 0.0
    for c in range(COLS):
        quad = constraint[0, COLS * col + c]
        linear = constraint[1, COLS * col + c]
        vr, vi = real[c], imag[c]
        ahead_real += weight * vr
        ahead_imag += weight * vi
        sum_real += weight * (quad * (vr * vr - vi * vi) + linear * vr)
        sum_imag += weight * (quad * (2.0 * vr * vi) + linear * vi)
        weight = weight * a1

    none = jnp.zeros((STEP, POINTS), jnp.float32)
    sum_real = jnp.concatenate((ahead_real[STEP:], none), axis=0) - sum_real
    sum_imag = jnp.concatenate((ahead_imag[STEP:], none), axis=0) - sum_imag
    edge = jnp.concatenate((ahead_real[:STEP], ahead_imag[:STEP]), axis=0)
    edge = jnp.where(row == 0, pltpu.roll(edge, POINTS - 1, 1), edge)
    for q in range(GROUPS):
        edge_out[q] = edge[:, 128 * q : 128 * q + 128]
        part_out[q, 0] = sum_real[:, 128 * q : 128 * q + 128]
        part_out[q, 1] = sum_imag[:, 128 * q : 128 * q + 128]

    def send_part(target):
        return pltpu.make_async_remote_copy(
            src_ref=part_out.at[target],
            dst_ref=part_in.at[col],
            send_sem=part_sem.at[0],
            recv_sem=part_sem.at[1],
            device_id=(row, target),
            device_id_type=MESH,
        )

    for i in range(1, GROUPS):
        send_part((col + i) % GROUPS).start()
    for q in range(GROUPS):
        pltpu.make_async_remote_copy(
            src_ref=edge_out.at[q],
            dst_ref=edge_in.at[col],
            send_sem=edge_sem.at[0],
            recv_sem=edge_sem.at[1],
            device_id=(previous, q),
            device_id_type=MESH,
        ).start()
    part_in[col] = part_out[col]

    point = lax.broadcasted_iota(jnp.int32, (BLOCK, 128), 0) % STEP
    theta = (shift + point.astype(jnp.float32)) * (TAU / STEP)
    van_real = jnp.cos(theta) - 1.0
    van_imag = jnp.sin(theta)
    denominator = van_real * van_real + van_imag * van_imag

    parts = pltpu.make_async_remote_copy(
        src_ref=part_out.at[pl.ds(0, GROUPS - 1)],
        dst_ref=part_in.at[pl.ds(0, GROUPS - 1)],
        send_sem=part_sem.at[0],
        recv_sem=part_sem.at[1],
        device_id=(partner, col),
        device_id_type=MESH,
    )
    edges = pltpu.make_async_remote_copy(
        src_ref=edge_out,
        dst_ref=edge_in,
        send_sem=edge_sem.at[0],
        recv_sem=edge_sem.at[1],
        device_id=(partner, col),
        device_id_type=MESH,
    )
    parts.wait_recv()
    edges.wait_recv()
    part = (part_in[0] + part_in[1]) + (part_in[2] + part_in[3])
    edge = (edge_in[0] + edge_in[1]) + (edge_in[2] + edge_in[3])
    none = jnp.zeros((BLOCK - STEP, 128), jnp.float32)
    num_real = part[0] + jnp.concatenate((none, edge[:STEP]), axis=0)
    num_imag = part[1] + jnp.concatenate((none, edge[STEP:]), axis=0)
    quotient[0] = (num_real * van_real + num_imag * van_imag) / denominator
    quotient[1] = (num_imag * van_real - num_real * van_imag) / denominator

    pair.wait_send()
    whole(0).wait_send()
    whole(1).wait_send()
    parts.wait_send()
    edges.wait_send()


def per_device(coeffs, constraint_coeffs, alpha, coset_shift):
    def pinned(array):
        return pltpu.with_memory_space_constraint(array, pltpu.HBM)

    tables = [pinned(jnp.asarray(table)) for table in (inner_table(), outer_table())]
    hbm = pl.BlockSpec(memory_space=pltpu.HBM)
    vmem = pl.BlockSpec(memory_space=pltpu.VMEM)
    smem = pl.BlockSpec(memory_space=pltpu.SMEM)
    f32 = jnp.float32
    bf16 = jnp.bfloat16
    return pl.pallas_call(
        kernel,
        out_shape=(
            jax.ShapeDtypeStruct((2, COLS, BLOCK, POINTS), f32),
            jax.ShapeDtypeStruct((2, BLOCK, 128), f32),
        ),
        in_specs=[hbm, hbm, smem, smem] + [hbm] * 2,
        out_specs=(vmem, vmem),
        scratch_shapes=[
            pltpu.VMEM((COLS, 4, K2), f32),
            pltpu.VMEM((COLS, 4, K2), f32),
            pltpu.VMEM((TILES, 2, K2, 256), bf16),
            pltpu.VMEM((2, 2, POINTS, 2 * POINTS), bf16),
            pltpu.VMEM((2, 2, 64, K2), bf16),
            pltpu.VMEM((2, TILES, 2, 8, 128), f32),
            pltpu.VMEM((2, HALF, 8, 128), f32),
            pltpu.VMEM((2, HALF, 8, 128), f32),
            pltpu.VMEM((GROUPS, 2, BLOCK, 128), f32),
            pltpu.VMEM((GROUPS, 2, BLOCK, 128), f32),
            pltpu.VMEM((GROUPS, 8, 128), f32),
            pltpu.VMEM((GROUPS, 8, 128), f32),
            pltpu.SemaphoreType.DMA((TILES + 1,)),
            pltpu.SemaphoreType.DMA,
            pltpu.SemaphoreType.DMA((2,)),
            pltpu.SemaphoreType.DMA((2,)),
            pltpu.SemaphoreType.DMA((2,)),
            pltpu.SemaphoreType.DMA((2,)),
            pltpu.SemaphoreType.DMA((2,)),
            pltpu.SMEM((2, GROUPS * COLS), f32),
            pltpu.SemaphoreType.DMA,
        ],
        compiler_params=pltpu.CompilerParams(
            collective_id=0, has_side_effects=True, vmem_limit_bytes=48 * 1024 * 1024
        ),
    )(
        pinned(coeffs),
        pinned(constraint_coeffs),
        alpha,
        coset_shift,
        *tables,
    )


def solution(mesh):
    in_specs = (P("col", "row", None), P(), P(), P())
    out_specs = (P(None, "col", "row", None), P(None, "row", "col"))
    return jax.shard_map(
        per_device, mesh=mesh, in_specs=in_specs, out_specs=out_specs, check_vma=False
    )
```

```python
import math

import jax
import jax.numpy as jnp
import ml_dtypes
import numpy as np
from jax import lax
from jax.experimental import pallas as pl
from jax.experimental.pallas import tpu as pltpu
from jax.sharding import PartitionSpec as P

MESH = pl.DeviceIdType.MESH
TAU = 2.0 * math.pi

COLS = 8
GROUPS = 4
ROWS = 128
HALF = 64
TILES = 8
K2 = 512
POINTS = 512
BLOCK = 16
STEP = 4
PEERS = HALF - 1
SOON_TILES = 3


def split_table(table):
    high = table.astype(np.float32).astype(ml_dtypes.bfloat16)
    low = (table - high.astype(np.float64)).astype(np.float32).astype(ml_dtypes.bfloat16)
    return high, low


def inner_table():
    k2 = np.arange(K2)[:, None]
    point = np.arange(1024)[None, :]
    angle = (k2 * point % 2048) * (TAU / 2048)
    cosine = np.cos(angle).reshape(K2, TILES, 128)
    sine = np.sin(angle).reshape(K2, TILES, 128)
    table = np.concatenate((cosine, sine), axis=2).transpose(1, 0, 2)
    return np.stack(split_table(table), axis=1)


def outer_table():
    place = np.arange(HALF)[:, None]
    low = np.arange(4)[None, :]
    k1 = np.stack([256 * part + 4 * place + low for part in range(2)])
    angle = (k1[..., None] * np.arange(POINTS) % POINTS) * (TAU / POINTS)
    cosine, sine = np.cos(angle), np.sin(angle)
    from_real = np.concatenate((cosine, sine), axis=3)
    from_imag = np.concatenate((-sine, cosine), axis=3)
    table = np.stack((from_real, from_imag), axis=2).reshape(2, 2 * 256, 2 * POINTS)
    return np.stack(split_table(table), axis=1)


def split(values):
    high = values.astype(jnp.bfloat16)
    return high, (values - high.astype(jnp.float32)).astype(jnp.bfloat16)


def dot(left, right):
    return jnp.dot(left, right, preferred_element_type=jnp.float32)


def swap_groups(pieces):
    lane = lax.broadcasted_iota(jnp.int32, pieces[0].shape, pieces[0].ndim - 1)
    axis = pieces[0].ndim - 1
    pieces = list(pieces)
    for bit in (4, 2, 1):
        keep = (lane // (16 * bit)) % 2 == 0
        for first in range(8):
            if first & bit:
                continue
            a, b = pieces[first], pieces[first + bit]
            pieces[first] = jnp.where(keep, a, pltpu.roll(b, 16 * bit, axis))
            pieces[first + bit] = jnp.where(keep, pltpu.roll(a, 128 - 16 * bit, axis), b)
    return pieces


def kernel(
    coeffs,
    constraint_hbm,
    alpha,
    coset,
    inner_hbm,
    outer_hbm,
    evaluations,
    quotient,
    own,
    other,
    inner,
    outer,
    x_split,
    twist,
    outgoing,
    incoming,
    part_out,
    part_in,
    edge_out,
    edge_in,
    table_sem,
    own_sem,
    pair_sem,
    send_sem,
    recv_sem,
    part_sem,
    edge_sem,
    constraint,
    small_sem,
    pair_ready,
    edge_ready,
    run_ready,
    extra,
    beyond,
    extra_sem,
):
    row = lax.axis_index("row")
    col = lax.axis_index("col")
    half = row // HALF
    place = row % HALF
    tile = place // 8
    core = place % 2
    base = half * HALF
    previous = (row + ROWS - 1) % ROWS
    following = (row + 1) % ROWS
    partner = (row + HALF) % ROWS

    barrier = pltpu.get_barrier_semaphore()

    def greet(device):
        pl.semaphore_signal(barrier, inc=1, device_id=device, device_id_type=MESH)

    def tile_of(i):
        offset = (1 + (3 + 3 * i) % 7) * (1 - i // 7)
        return (tile + offset * (1 - 2 * core) + 8) % TILES

    def load_tile(t):
        return pltpu.make_async_copy(inner_hbm.at[t], inner.at[t], table_sem.at[t])

    load_own = pltpu.make_async_copy(coeffs, own, own_sem)
    load_own.start()
    load_small = pltpu.make_async_copy(constraint_hbm, constraint, small_sem)
    load_small.start()

    @pl.loop(0, TILES)
    def _(i):
        load_tile(tile_of(i)).start()

    load_outer = pltpu.make_async_copy(outer_hbm, outer, table_sem.at[TILES])
    load_outer.start()

    first_half = half == 0
    first_row = row == 0
    last_row = row == ROWS - 1

    @pl.when(first_half)
    def _():
        greet((partner, col))

    seat = place % 8

    def in_line(i):
        return base + (tile + i) % TILES * 8 + seat

    for i in range(1, TILES):
        greet((base + 8 * tile + (place + i) % 8, col))
        greet((in_line(i), col))
    for i in range(1, GROUPS):
        greet((row, (col + i) % GROUPS))

    @pl.when((row != PEERS) & (row != ROWS - 1))
    def _():
        for i in range(GROUPS):
            greet((following, i))

    @pl.when(first_row)
    def _():
        for i in range(GROUPS):
            greet((previous, i))

    expected = 2 * (TILES - 1) + GROUPS - 1 + half
    expected = expected + jnp.where(place == 0, 0, GROUPS) + jnp.where(last_row, GROUPS, 0)

    shift = coset[0]
    k2 = lax.broadcasted_iota(jnp.int32, (1, K2), 1)
    phase = k2.astype(jnp.float32) * (shift * (TAU / 2048))
    sign = (1 - 2 * ((k2 % 2) * half)).astype(jnp.float32)
    turn = (1 - 2 * (k2 % 2)).astype(jnp.float32)
    phase_cos = jnp.cos(phase) * sign
    phase_sin = jnp.sin(phase) * sign

    wide = 128 * (TILES + 1)
    sub = lax.broadcasted_iota(jnp.int32, (8, wide), 0)
    k1 = 256 * ((half + sub // 4) % 2) + 4 * place + sub % 4
    point = 1024 * half + lax.broadcasted_iota(jnp.int32, (8, wide), 1)
    k1_f = k1.astype(jnp.float32)
    angle = ((k1 * point).astype(jnp.float32) + k1_f * shift) * (TAU / 1048576)
    cosine, sine = jnp.cos(angle), jnp.sin(angle)
    cosine_turned, sine_turned = pltpu.roll(cosine, 4, 0), pltpu.roll(sine, 4, 0)
    upper = sub < 4
    pairs = (
        (jnp.where(upper, cosine, cosine_turned), jnp.where(upper, -sine, sine_turned)),
        (jnp.where(upper, cosine_turned, cosine), jnp.where(upper, -sine_turned, sine)),
    )
    for p in range(2):
        for t in range(TILES + 1):
            twist[p, t, 0] = pairs[p][0][:, 128 * t : 128 * t + 128]
            twist[p, t, 1] = pairs[p][1][:, 128 * t : 128 * t + 128]

    def prepare(p, source):
        x = source[...]
        x = jnp.concatenate((x * phase_cos, x * phase_sin), axis=1).reshape(64, K2)
        high, low = split(x)
        x_split[p, 0] = high
        x_split[p, 1] = low
        high, low = split(x * turn)
        x_split[2 + p, 0] = high
        x_split[2 + p, 1] = low

    load_own.wait()
    prepare(0, own)
    pl.semaphore_wait(barrier, expected)

    pair = pltpu.make_async_remote_copy(
        src_ref=coeffs,
        dst_ref=other,
        send_sem=pair_sem.at[0],
        recv_sem=pair_sem.at[1],
        device_id=(partner, col),
        device_id_type=MESH,
    )

    @pl.when(half == 1)
    def _():
        pl.semaphore_signal(pair_ready, inc=1, device_id=(partner, col), device_id_type=MESH)
        pair.start()

    for i in range(1, TILES):
        pl.semaphore_signal(run_ready, inc=1, device_id=(in_line(i), col), device_id_type=MESH)

    @pl.when(last_row)
    def _():
        for i in range(GROUPS):
            pl.semaphore_signal(edge_ready, inc=1, device_id=(following, i), device_id_type=MESH)

    def send(source, target, device, sem):
        return pltpu.make_async_remote_copy(
            src_ref=source,
            dst_ref=target,
            send_sem=send_sem.at[sem],
            recv_sem=recv_sem.at[sem],
            device_id=(base + device, col),
            device_id_type=MESH,
        )

    def send_extra(part):
        return pltpu.make_async_remote_copy(
            src_ref=outgoing.at[HALF, part],
            dst_ref=extra.at[place, part],
            send_sem=extra_sem.at[0, part],
            recv_sem=extra_sem.at[1, 0],
            device_id=(base + PEERS, col),
            device_id_type=MESH,
        )

    def blocks(sem):
        where = (pl.ds(0, PEERS), 0)
        return send(outgoing.at[where], incoming.at[where], (place + 1) % HALF, sem)

    minus = jnp.where(lax.broadcasted_iota(jnp.int32, (1, 8, 128), 1) < 4, -1.0, 1.0)

    def tile_blocks(x, t, p, turned):
        ah, al = x_split[x, 0], x_split[x, 1]
        bh, bl = inner[t, 0], inner[t, 1]
        y = dot(ah, bh) + (dot(al, bh) + dot(ah, bl))
        z = y[:, :128].reshape(COLS, 8, 128)
        z = z + minus * pltpu.roll(y[:, 128:].reshape(COLS, 8, 128), 4, 1)
        z = z * twist[p, turned, 0][None] + pltpu.roll(z, 4, 1) * twist[p, turned, 1][None]
        return swap_groups([z[c] for c in range(COLS)])

    def run_tile(p, t):
        for d, block in enumerate(tile_blocks(p, t, p, t)):
            outgoing[8 * t + d, (half + p) % 2] = block

    def send_tile(p, t, first):
        part = (half + p) % 2
        for j in range(first, 8):
            device = 8 * t + (place + j) % 8
            send(outgoing.at[device, part], incoming.at[place, part], device, p).start()

    def extra_tile(p):
        part = (half + p) % 2
        outgoing[HALF, part] = tile_blocks(2 + p, 0, p, TILES)[0]

        @pl.when(place < PEERS)
        def _():
            send_extra(part).start()

    pl.semaphore_wait(run_ready, TILES - 1)

    def own_tile(i):
        t = tile_of(i)
        load_tile(t).wait()
        run_tile(0, t)
        send_tile(0, t, 0)

    pl.loop(0, SOON_TILES)(own_tile)

    @pl.when(first_half)
    def _():
        pl.semaphore_wait(pair_ready, 1)
        pair.start()

    pl.loop(SOON_TILES, TILES - 1)(own_tile)
    load_tile(tile).wait()
    run_tile(0, tile)
    send_tile(0, tile, 1)

    @pl.when(first_half)
    def _():
        extra_tile(0)

    pair.wait_recv()
    prepare(1, other)

    @pl.loop(0, TILES - 1)
    def _(i):
        t = tile_of(i)
        run_tile(1, t)
        send_tile(1, t, 0)

    @pl.when(first_half)
    def _():
        extra_tile(1)

    run_tile(1, tile)
    send_tile(1, tile, 1)
    incoming[place] = outgoing[place]
    load_outer.wait()

    def finish(blocks_in, part):
        held = blocks_in[:, part].reshape(POINTS, 128).T
        rh, rl = split(held)
        th, tl = outer[part, 0], outer[part, 1]
        return dot(rh, th) + (dot(rl, th) + dot(rh, tl))

    @pl.when(half == 1)
    def _():
        blocks(1).wait_recv()

    @pl.when(first_half)
    def _():
        blocks(0).wait_recv()

    v = finish(incoming, 0)

    @pl.when(half == 1)
    def _():
        blocks(0).wait_recv()

    @pl.when(first_half)
    def _():
        blocks(1).wait_recv()

    v = v + finish(incoming, 1)
    real = v[:, :POINTS].reshape(COLS, BLOCK, POINTS)
    imag = v[:, POINTS:].reshape(COLS, BLOCK, POINTS)
    evaluations[0] = real
    evaluations[1] = imag

    load_small.wait()
    a1 = alpha[0]
    a2 = a1 * a1
    a4 = a2 * a2
    a8 = a4 * a4
    weight = jnp.where(col % 2 == 1, a8, 1.0) * jnp.where(col // 2 == 1, a8 * a8, 1.0)
    first_weight = weight
    ahead_real = ahead_imag = sum_real = sum_imag = 0.0
    for c in range(COLS):
        quad = constraint[0, COLS * col + c]
        linear = constraint[1, COLS * col + c]
        vr, vi = real[c], imag[c]
        ahead_real += weight * vr
        ahead_imag += weight * vi
        sum_real += weight * (quad * (vr * vr - vi * vi) + linear * vr)
        sum_imag += weight * (quad * (2.0 * vr * vi) + linear * vi)
        weight = weight * a1

    beyond[...] = jnp.zeros((2, STEP, POINTS), jnp.float32)

    @pl.when(row == PEERS)
    def _():
        extra[place] = outgoing[HALF]
        received = pltpu.make_async_remote_copy(
            src_ref=outgoing.at[pl.ds(0, PEERS)],
            dst_ref=extra.at[pl.ds(0, PEERS)],
            send_sem=extra_sem.at[0, 0],
            recv_sem=extra_sem.at[1, 0],
            device_id=(base, col),
            device_id_type=MESH,
        )
        received.wait_recv()
        u = finish(extra, 0) + finish(extra, 1)
        edge_in[...] = jnp.zeros((GROUPS, 8, 128), jnp.float32)
        scale = first_weight
        for c in range(COLS):
            for p in range(2):
                found = u[BLOCK * c : BLOCK * c + 8, POINTS * p : POINTS * (p + 1)]
                beyond[p] += scale * found[:STEP]
            scale = scale * a1

    sum_real = jnp.concatenate((ahead_real[STEP:], beyond[0]), axis=0) - sum_real
    sum_imag = jnp.concatenate((ahead_imag[STEP:], beyond[1]), axis=0) - sum_imag
    edge = jnp.concatenate((ahead_real[:STEP], ahead_imag[:STEP]), axis=0)
    edge = jnp.where(row == 0, pltpu.roll(edge, POINTS - 1, 1), edge)
    for q in range(GROUPS):
        edge_out[q] = edge[:, 128 * q : 128 * q + 128]
        part_out[q, 0] = sum_real[:, 128 * q : 128 * q + 128]
        part_out[q, 1] = sum_imag[:, 128 * q : 128 * q + 128]

    def send_part(target):
        return pltpu.make_async_remote_copy(
            src_ref=part_out.at[target],
            dst_ref=part_in.at[col],
            send_sem=part_sem.at[0],
            recv_sem=part_sem.at[1],
            device_id=(row, target),
            device_id_type=MESH,
        )

    for i in range(1, GROUPS):
        send_part((col + i) % GROUPS).start()

    @pl.when(first_row)
    def _():
        pl.semaphore_wait(edge_ready, GROUPS)

    @pl.when(row != HALF)
    def _():
        for q in range(GROUPS):
            pltpu.make_async_remote_copy(
                src_ref=edge_out.at[q],
                dst_ref=edge_in.at[col],
                send_sem=edge_sem.at[0],
                recv_sem=edge_sem.at[1],
                device_id=(previous, q),
                device_id_type=MESH,
            ).start()

    part_in[col] = part_out[col]

    point = lax.broadcasted_iota(jnp.int32, (BLOCK, 128), 0) % STEP
    theta = (shift + point.astype(jnp.float32)) * (TAU / STEP)
    van_real = jnp.cos(theta) - 1.0
    van_imag = jnp.sin(theta)
    denominator = van_real * van_real + van_imag * van_imag

    parts = pltpu.make_async_remote_copy(
        src_ref=part_out.at[pl.ds(0, GROUPS - 1)],
        dst_ref=part_in.at[pl.ds(0, GROUPS - 1)],
        send_sem=part_sem.at[0],
        recv_sem=part_sem.at[1],
        device_id=(partner, col),
        device_id_type=MESH,
    )
    edges = pltpu.make_async_remote_copy(
        src_ref=edge_out,
        dst_ref=edge_in,
        send_sem=edge_sem.at[0],
        recv_sem=edge_sem.at[1],
        device_id=(partner, col),
        device_id_type=MESH,
    )
    parts.wait_recv()

    @pl.when(row != PEERS)
    def _():
        edges.wait_recv()

    part = (part_in[0] + part_in[1]) + (part_in[2] + part_in[3])
    edge = (edge_in[0] + edge_in[1]) + (edge_in[2] + edge_in[3])
    none = jnp.zeros((BLOCK - STEP, 128), jnp.float32)
    num_real = part[0] + jnp.concatenate((none, edge[:STEP]), axis=0)
    num_imag = part[1] + jnp.concatenate((none, edge[STEP:]), axis=0)
    quotient[0] = (num_real * van_real + num_imag * van_imag) / denominator
    quotient[1] = (num_imag * van_real - num_real * van_imag) / denominator

    pair.wait_send()
    blocks(0).wait_send()
    blocks(1).wait_send()

    @pl.when(first_half & (place < PEERS))
    def _():
        send_extra(0).wait_send()
        send_extra(1).wait_send()

    parts.wait_send()

    @pl.when(row != HALF)
    def _():
        edges.wait_send()


def per_device(coeffs, constraint_coeffs, alpha, coset_shift):
    def pinned(array):
        return pltpu.with_memory_space_constraint(array, pltpu.HBM)

    tables = [pinned(jnp.asarray(table)) for table in (inner_table(), outer_table())]
    hbm = pl.BlockSpec(memory_space=pltpu.HBM)
    vmem = pl.BlockSpec(memory_space=pltpu.VMEM)
    smem = pl.BlockSpec(memory_space=pltpu.SMEM)
    f32 = jnp.float32
    bf16 = jnp.bfloat16
    return pl.pallas_call(
        kernel,
        out_shape=(
            jax.ShapeDtypeStruct((2, COLS, BLOCK, POINTS), f32),
            jax.ShapeDtypeStruct((2, BLOCK, 128), f32),
        ),
        in_specs=[hbm, hbm, smem, smem] + [hbm] * 2,
        out_specs=(vmem, vmem),
        scratch_shapes=[
            pltpu.VMEM((COLS, 4, K2), f32),
            pltpu.VMEM((COLS, 4, K2), f32),
            pltpu.VMEM((TILES, 2, K2, 256), bf16),
            pltpu.VMEM((2, 2, POINTS, 2 * POINTS), bf16),
            pltpu.VMEM((4, 2, 64, K2), bf16),
            pltpu.VMEM((2, TILES + 1, 2, 8, 128), f32),
            pltpu.VMEM((HALF + 1, 2, 8, 128), f32),
            pltpu.VMEM((HALF, 2, 8, 128), f32),
            pltpu.VMEM((GROUPS, 2, BLOCK, 128), f32),
            pltpu.VMEM((GROUPS, 2, BLOCK, 128), f32),
            pltpu.VMEM((GROUPS, 8, 128), f32),
            pltpu.VMEM((GROUPS, 8, 128), f32),
            pltpu.SemaphoreType.DMA((TILES + 1,)),
            pltpu.SemaphoreType.DMA,
            pltpu.SemaphoreType.DMA((2,)),
            pltpu.SemaphoreType.DMA((2,)),
            pltpu.SemaphoreType.DMA((2,)),
            pltpu.SemaphoreType.DMA((2,)),
            pltpu.SemaphoreType.DMA((2,)),
            pltpu.SMEM((2, GROUPS * COLS), f32),
            pltpu.SemaphoreType.DMA,
            pltpu.SemaphoreType.REGULAR,
            pltpu.SemaphoreType.REGULAR,
            pltpu.SemaphoreType.REGULAR,
            pltpu.VMEM((HALF, 2, 8, 128), f32),
            pltpu.VMEM((2, STEP, POINTS), f32),
            pltpu.SemaphoreType.DMA((2, 2)),
        ],
        compiler_params=pltpu.CompilerParams(
            collective_id=0, has_side_effects=True, vmem_limit_bytes=48 * 1024 * 1024
        ),
    )(
        pinned(coeffs),
        pinned(constraint_coeffs),
        alpha,
        coset_shift,
        *tables,
    )


def solution(mesh):
    in_specs = (P("col", "row", None), P(), P(), P())
    out_specs = (P(None, "col", "row", None), P(None, "row", "col"))
    return jax.shard_map(
        per_device, mesh=mesh, in_specs=in_specs, out_specs=out_specs, check_vma=False
    )
```

```python
import math

import jax
import jax.numpy as jnp
import ml_dtypes
import numpy as np
from jax import lax
from jax.experimental import pallas as pl
from jax.experimental.pallas import tpu as pltpu
from jax.sharding import PartitionSpec as P

MESH = pl.DeviceIdType.MESH
TAU = 2.0 * math.pi

COLS = 8
GROUPS = 4
ROWS = 128
HALF = 64
TILES = 8
K2 = 512
POINTS = 512
BLOCK = 16
STEP = 4
PEERS = HALF - 1


def split_table(table):
    high = table.astype(np.float32).astype(ml_dtypes.bfloat16)
    low = (table - high.astype(np.float64)).astype(np.float32).astype(ml_dtypes.bfloat16)
    return high, low


def inner_table():
    k2 = np.arange(K2)[:, None]
    point = np.arange(1024)[None, :]
    angle = (k2 * point % 2048) * (TAU / 2048)
    cosine = np.cos(angle).reshape(K2, TILES, 128)
    sine = np.sin(angle).reshape(K2, TILES, 128)
    table = np.concatenate((cosine, sine), axis=2).transpose(1, 0, 2)
    return np.stack(split_table(table), axis=1)


def outer_table():
    place = np.arange(HALF)[:, None]
    low = np.arange(4)[None, :]
    k1 = np.stack([256 * part + 4 * place + low for part in range(2)])
    angle = (k1[..., None] * np.arange(POINTS) % POINTS) * (TAU / POINTS)
    cosine, sine = np.cos(angle), np.sin(angle)
    from_real = np.concatenate((cosine, sine), axis=3)
    from_imag = np.concatenate((-sine, cosine), axis=3)
    table = np.stack((from_real, from_imag), axis=2).reshape(2, 2 * 256, 2 * POINTS)
    return np.stack(split_table(table), axis=1)


def split(values):
    high = values.astype(jnp.bfloat16)
    return high, (values - high.astype(jnp.float32)).astype(jnp.bfloat16)


def dot(left, right):
    return jnp.dot(left, right, preferred_element_type=jnp.float32)


def swap_groups(pieces):
    lane = lax.broadcasted_iota(jnp.int32, pieces[0].shape, pieces[0].ndim - 1)
    axis = pieces[0].ndim - 1
    pieces = list(pieces)
    for bit in (4, 2, 1):
        keep = (lane // (16 * bit)) % 2 == 0
        for first in range(8):
            if first & bit:
                continue
            a, b = pieces[first], pieces[first + bit]
            pieces[first] = jnp.where(keep, a, pltpu.roll(b, 16 * bit, axis))
            pieces[first + bit] = jnp.where(keep, pltpu.roll(a, 128 - 16 * bit, axis), b)
    return pieces


def kernel(
    coeffs,
    constraint_hbm,
    alpha,
    coset,
    inner_hbm,
    outer_hbm,
    evaluations,
    quotient,
    own,
    other,
    inner,
    outer,
    x_split,
    twist,
    outgoing,
    incoming,
    part_out,
    part_in,
    edge_out,
    edge_in,
    table_sem,
    own_sem,
    pair_sem,
    send_sem,
    recv_sem,
    part_sem,
    edge_sem,
    constraint,
    small_sem,
    pair_ready,
    edge_ready,
    run_ready,
    extra,
    beyond,
    extra_sem,
):
    row = lax.axis_index("row")
    col = lax.axis_index("col")
    half = row // HALF
    place = row % HALF
    tile = place // 8
    core = place % 2
    base = half * HALF
    previous = (row + ROWS - 1) % ROWS
    following = (row + 1) % ROWS
    partner = (row + HALF) % ROWS

    barrier = pltpu.get_barrier_semaphore()

    def greet(device):
        pl.semaphore_signal(barrier, inc=1, device_id=device, device_id_type=MESH)

    def tile_of(i):
        offset = (1 + (3 + 3 * i) % 7) * (1 - i // 7)
        return (tile + offset * (1 - 2 * core) + 8) % TILES

    def load_tile(t):
        return pltpu.make_async_copy(inner_hbm.at[t], inner.at[t], table_sem.at[t])

    load_own = pltpu.make_async_copy(coeffs, own, own_sem)
    load_own.start()
    load_small = pltpu.make_async_copy(constraint_hbm, constraint, small_sem)
    load_small.start()

    @pl.loop(0, TILES)
    def _(i):
        load_tile(tile_of(i)).start()

    load_outer = pltpu.make_async_copy(outer_hbm, outer, table_sem.at[TILES])
    load_outer.start()

    first_half = half == 0
    first_row = row == 0
    last_row = row == ROWS - 1

    @pl.when(first_half)
    def _():
        greet((partner, col))

    seat = place % 8

    def in_line(i):
        return base + (tile + i) % TILES * 8 + seat

    for i in range(1, TILES):
        greet((base + 8 * tile + (place + i) % 8, col))
        greet((in_line(i), col))
    for i in range(1, GROUPS):
        greet((row, (col + i) % GROUPS))

    @pl.when((row != PEERS) & (row != ROWS - 1))
    def _():
        for i in range(GROUPS):
            greet((following, i))

    @pl.when(first_row)
    def _():
        for i in range(GROUPS):
            greet((previous, i))

    expected = 2 * (TILES - 1) + GROUPS - 1 + half
    expected = expected + jnp.where(place == 0, 0, GROUPS) + jnp.where(last_row, GROUPS, 0)

    shift = coset[0]
    k2 = lax.broadcasted_iota(jnp.int32, (1, K2), 1)
    phase = k2.astype(jnp.float32) * (shift * (TAU / 2048))
    sign = (1 - 2 * ((k2 % 2) * half)).astype(jnp.float32)
    turn = (1 - 2 * (k2 % 2)).astype(jnp.float32)
    phase_cos = jnp.cos(phase) * sign
    phase_sin = jnp.sin(phase) * sign

    wide = 128 * (TILES + 1)
    sub = lax.broadcasted_iota(jnp.int32, (8, wide), 0)
    k1 = 256 * ((half + sub // 4) % 2) + 4 * place + sub % 4
    point = 1024 * half + lax.broadcasted_iota(jnp.int32, (8, wide), 1)
    k1_f = k1.astype(jnp.float32)
    angle = ((k1 * point).astype(jnp.float32) + k1_f * shift) * (TAU / 1048576)
    cosine, sine = jnp.cos(angle), jnp.sin(angle)
    cosine_turned, sine_turned = pltpu.roll(cosine, 4, 0), pltpu.roll(sine, 4, 0)
    upper = sub < 4
    pairs = (
        (jnp.where(upper, cosine, cosine_turned), jnp.where(upper, -sine, sine_turned)),
        (jnp.where(upper, cosine_turned, cosine), jnp.where(upper, -sine_turned, sine)),
    )
    for p in range(2):
        for t in range(TILES + 1):
            twist[p, t, 0] = pairs[p][0][:, 128 * t : 128 * t + 128]
            twist[p, t, 1] = pairs[p][1][:, 128 * t : 128 * t + 128]

    def prepare(p, source):
        x = source[...]
        x = jnp.concatenate((x * phase_cos, x * phase_sin), axis=1).reshape(64, K2)
        high, low = split(x)
        x_split[p, 0] = high
        x_split[p, 1] = low
        high, low = split(x * turn)
        x_split[2 + p, 0] = high
        x_split[2 + p, 1] = low

    load_own.wait()
    prepare(0, own)
    pl.semaphore_wait(barrier, expected)

    pair = pltpu.make_async_remote_copy(
        src_ref=coeffs,
        dst_ref=other,
        send_sem=pair_sem.at[0],
        recv_sem=pair_sem.at[1],
        device_id=(partner, col),
        device_id_type=MESH,
    )

    @pl.when(half == 1)
    def _():
        pl.semaphore_signal(pair_ready, inc=1, device_id=(partner, col), device_id_type=MESH)
        pair.start()

    for i in range(1, TILES):
        pl.semaphore_signal(run_ready, inc=1, device_id=(in_line(i), col), device_id_type=MESH)

    @pl.when(last_row)
    def _():
        for i in range(GROUPS):
            pl.semaphore_signal(edge_ready, inc=1, device_id=(following, i), device_id_type=MESH)

    def send(source, target, device, sem):
        return pltpu.make_async_remote_copy(
            src_ref=source,
            dst_ref=target,
            send_sem=send_sem.at[sem],
            recv_sem=recv_sem.at[sem],
            device_id=(base + device, col),
            device_id_type=MESH,
        )

    def send_extra(part):
        return pltpu.make_async_remote_copy(
            src_ref=outgoing.at[HALF, part],
            dst_ref=extra.at[place, part],
            send_sem=extra_sem.at[0, part],
            recv_sem=extra_sem.at[1, 0],
            device_id=(base + PEERS, col),
            device_id_type=MESH,
        )

    def blocks(sem):
        where = (pl.ds(0, PEERS), 0)
        return send(outgoing.at[where], incoming.at[where], (place + 1) % HALF, sem)

    minus = jnp.where(lax.broadcasted_iota(jnp.int32, (1, 8, 128), 1) < 4, -1.0, 1.0)

    def tile_blocks(x, t, p, turned):
        ah, al = x_split[x, 0], x_split[x, 1]
        bh, bl = inner[t, 0], inner[t, 1]
        y = dot(ah, bh) + (dot(al, bh) + dot(ah, bl))
        z = y[:, :128].reshape(COLS, 8, 128)
        z = z + minus * pltpu.roll(y[:, 128:].reshape(COLS, 8, 128), 4, 1)
        z = z * twist[p, turned, 0][None] + pltpu.roll(z, 4, 1) * twist[p, turned, 1][None]
        return swap_groups([z[c] for c in range(COLS)])

    def run_tile(p, t):
        for d, block in enumerate(tile_blocks(p, t, p, t)):
            outgoing[8 * t + d, (half + p) % 2] = block

    def send_tile(p, t, first):
        part = (half + p) % 2
        for j in range(first, 8):
            device = 8 * t + (place + j) % 8
            send(outgoing.at[device, part], incoming.at[place, part], device, p).start()

    def extra_tile(p):
        part = (half + p) % 2
        outgoing[HALF, part] = tile_blocks(2 + p, 0, p, TILES)[0]

        @pl.when(place < PEERS)
        def _():
            send_extra(part).start()

    pl.semaphore_wait(run_ready, TILES - 1)

    def own_tile(i):
        t = tile_of(i)
        load_tile(t).wait()
        run_tile(0, t)
        send_tile(0, t, 0)

    pl.loop(0, TILES - 1)(own_tile)
    load_tile(tile).wait()
    run_tile(0, tile)
    send_tile(0, tile, 1)

    @pl.when(first_half)
    def _():
        extra_tile(0)
        pl.semaphore_wait(pair_ready, 1)
        pair.start()

    pair.wait_recv()
    prepare(1, other)

    @pl.loop(0, TILES - 1)
    def _(i):
        t = tile_of(i)
        run_tile(1, t)
        send_tile(1, t, 0)

    run_tile(1, tile)
    send_tile(1, tile, 1)

    @pl.when(first_half)
    def _():
        extra_tile(1)

    incoming[place] = outgoing[place]
    load_outer.wait()

    def finish(blocks_in, part):
        held = blocks_in[:, part].reshape(POINTS, 128).T
        rh, rl = split(held)
        th, tl = outer[part, 0], outer[part, 1]
        return dot(rh, th) + (dot(rl, th) + dot(rh, tl))

    @pl.when(half == 1)
    def _():
        blocks(1).wait_recv()

    @pl.when(first_half)
    def _():
        blocks(0).wait_recv()

    v = finish(incoming, 0)

    @pl.when(half == 1)
    def _():
        blocks(0).wait_recv()

    @pl.when(first_half)
    def _():
        blocks(1).wait_recv()

    v = v + finish(incoming, 1)
    real = v[:, :POINTS].reshape(COLS, BLOCK, POINTS)
    imag = v[:, POINTS:].reshape(COLS, BLOCK, POINTS)

    load_small.wait()
    a1 = alpha[0]
    a2 = a1 * a1
    a4 = a2 * a2
    a8 = a4 * a4
    weight = jnp.where(col % 2 == 1, a8, 1.0) * jnp.where(col // 2 == 1, a8 * a8, 1.0)
    first_weight = weight
    ahead_real = ahead_imag = sum_real = sum_imag = 0.0
    for c in range(COLS):
        quad = constraint[0, COLS * col + c]
        linear = constraint[1, COLS * col + c]
        vr, vi = real[c], imag[c]
        ahead_real += weight * vr
        ahead_imag += weight * vi
        sum_real += weight * (quad * (vr * vr - vi * vi) + linear * vr)
        sum_imag += weight * (quad * (2.0 * vr * vi) + linear * vi)
        weight = weight * a1

    beyond[...] = jnp.zeros((2, STEP, POINTS), jnp.float32)

    @pl.when(row == PEERS)
    def _():
        extra[place] = outgoing[HALF]
        received = pltpu.make_async_remote_copy(
            src_ref=outgoing.at[pl.ds(0, PEERS)],
            dst_ref=extra.at[pl.ds(0, PEERS)],
            send_sem=extra_sem.at[0, 0],
            recv_sem=extra_sem.at[1, 0],
            device_id=(base, col),
            device_id_type=MESH,
        )
        received.wait_recv()
        u = finish(extra, 0) + finish(extra, 1)
        edge_in[...] = jnp.zeros((GROUPS, 8, 128), jnp.float32)
        scale = first_weight
        for c in range(COLS):
            for p in range(2):
                found = u[BLOCK * c : BLOCK * c + 8, POINTS * p : POINTS * (p + 1)]
                beyond[p] += scale * found[:STEP]
            scale = scale * a1

    sum_real = jnp.concatenate((ahead_real[STEP:], beyond[0]), axis=0) - sum_real
    sum_imag = jnp.concatenate((ahead_imag[STEP:], beyond[1]), axis=0) - sum_imag
    edge = jnp.concatenate((ahead_real[:STEP], ahead_imag[:STEP]), axis=0)
    edge = jnp.where(row == 0, pltpu.roll(edge, POINTS - 1, 1), edge)
    for q in range(GROUPS):
        edge_out[q] = edge[:, 128 * q : 128 * q + 128]
        part_out[q, 0] = sum_real[:, 128 * q : 128 * q + 128]
        part_out[q, 1] = sum_imag[:, 128 * q : 128 * q + 128]

    def send_part(target):
        return pltpu.make_async_remote_copy(
            src_ref=part_out.at[target],
            dst_ref=part_in.at[col],
            send_sem=part_sem.at[0],
            recv_sem=part_sem.at[1],
            device_id=(row, target),
            device_id_type=MESH,
        )

    for i in range(1, GROUPS):
        send_part((col + i) % GROUPS).start()

    @pl.when(first_row)
    def _():
        pl.semaphore_wait(edge_ready, GROUPS)

    @pl.when(row != HALF)
    def _():
        for q in range(GROUPS):
            pltpu.make_async_remote_copy(
                src_ref=edge_out.at[q],
                dst_ref=edge_in.at[col],
                send_sem=edge_sem.at[0],
                recv_sem=edge_sem.at[1],
                device_id=(previous, q),
                device_id_type=MESH,
            ).start()

    part_in[col] = part_out[col]
    evaluations[0] = real
    evaluations[1] = imag

    point = lax.broadcasted_iota(jnp.int32, (BLOCK, 128), 0) % STEP
    theta = (shift + point.astype(jnp.float32)) * (TAU / STEP)
    van_real = jnp.cos(theta) - 1.0
    van_imag = jnp.sin(theta)
    denominator = van_real * van_real + van_imag * van_imag

    parts = pltpu.make_async_remote_copy(
        src_ref=part_out.at[pl.ds(0, GROUPS - 1)],
        dst_ref=part_in.at[pl.ds(0, GROUPS - 1)],
        send_sem=part_sem.at[0],
        recv_sem=part_sem.at[1],
        device_id=(partner, col),
        device_id_type=MESH,
    )
    edges = pltpu.make_async_remote_copy(
        src_ref=edge_out,
        dst_ref=edge_in,
        send_sem=edge_sem.at[0],
        recv_sem=edge_sem.at[1],
        device_id=(partner, col),
        device_id_type=MESH,
    )
    parts.wait_recv()

    @pl.when(row != PEERS)
    def _():
        edges.wait_recv()

    part = (part_in[0] + part_in[1]) + (part_in[2] + part_in[3])
    edge = (edge_in[0] + edge_in[1]) + (edge_in[2] + edge_in[3])
    none = jnp.zeros((BLOCK - STEP, 128), jnp.float32)
    num_real = part[0] + jnp.concatenate((none, edge[:STEP]), axis=0)
    num_imag = part[1] + jnp.concatenate((none, edge[STEP:]), axis=0)
    quotient[0] = (num_real * van_real + num_imag * van_imag) / denominator
    quotient[1] = (num_imag * van_real - num_real * van_imag) / denominator

    pair.wait_send()
    blocks(0).wait_send()
    blocks(1).wait_send()

    @pl.when(first_half & (place < PEERS))
    def _():
        send_extra(0).wait_send()
        send_extra(1).wait_send()

    parts.wait_send()

    @pl.when(row != HALF)
    def _():
        edges.wait_send()


def per_device(coeffs, constraint_coeffs, alpha, coset_shift):
    def pinned(array):
        return pltpu.with_memory_space_constraint(array, pltpu.HBM)

    tables = [pinned(jnp.asarray(table)) for table in (inner_table(), outer_table())]
    hbm = pl.BlockSpec(memory_space=pltpu.HBM)
    vmem = pl.BlockSpec(memory_space=pltpu.VMEM)
    smem = pl.BlockSpec(memory_space=pltpu.SMEM)
    f32 = jnp.float32
    bf16 = jnp.bfloat16
    return pl.pallas_call(
        kernel,
        out_shape=(
            jax.ShapeDtypeStruct((2, COLS, BLOCK, POINTS), f32),
            jax.ShapeDtypeStruct((2, BLOCK, 128), f32),
        ),
        in_specs=[hbm, hbm, smem, smem] + [hbm] * 2,
        out_specs=(vmem, vmem),
        scratch_shapes=[
            pltpu.VMEM((COLS, 4, K2), f32),
            pltpu.VMEM((COLS, 4, K2), f32),
            pltpu.VMEM((TILES, 2, K2, 256), bf16),
            pltpu.VMEM((2, 2, POINTS, 2 * POINTS), bf16),
            pltpu.VMEM((4, 2, 64, K2), bf16),
            pltpu.VMEM((2, TILES + 1, 2, 8, 128), f32),
            pltpu.VMEM((HALF + 1, 2, 8, 128), f32),
            pltpu.VMEM((HALF, 2, 8, 128), f32),
            pltpu.VMEM((GROUPS, 2, BLOCK, 128), f32),
            pltpu.VMEM((GROUPS, 2, BLOCK, 128), f32),
            pltpu.VMEM((GROUPS, 8, 128), f32),
            pltpu.VMEM((GROUPS, 8, 128), f32),
            pltpu.SemaphoreType.DMA((TILES + 1,)),
            pltpu.SemaphoreType.DMA,
            pltpu.SemaphoreType.DMA((2,)),
            pltpu.SemaphoreType.DMA((2,)),
            pltpu.SemaphoreType.DMA((2,)),
            pltpu.SemaphoreType.DMA((2,)),
            pltpu.SemaphoreType.DMA((2,)),
            pltpu.SMEM((2, GROUPS * COLS), f32),
            pltpu.SemaphoreType.DMA,
            pltpu.SemaphoreType.REGULAR,
            pltpu.SemaphoreType.REGULAR,
            pltpu.SemaphoreType.REGULAR,
            pltpu.VMEM((HALF, 2, 8, 128), f32),
            pltpu.VMEM((2, STEP, POINTS), f32),
            pltpu.SemaphoreType.DMA((2, 2)),
        ],
        compiler_params=pltpu.CompilerParams(
            collective_id=0, has_side_effects=True, vmem_limit_bytes=48 * 1024 * 1024
        ),
    )(
        pinned(coeffs),
        pinned(constraint_coeffs),
        alpha,
        coset_shift,
        *tables,
    )


def solution(mesh):
    in_specs = (P("col", "row", None), P(), P(), P())
    out_specs = (P(None, "col", "row", None), P(None, "row", "col"))
    return jax.shard_map(
        per_device, mesh=mesh, in_specs=in_specs, out_specs=out_specs, check_vma=False
    )
```

```python
import math

import jax
import jax.numpy as jnp
import ml_dtypes
import numpy as np
from jax import lax
from jax.experimental import pallas as pl
from jax.experimental.pallas import tpu as pltpu
from jax.sharding import PartitionSpec as P

MESH = pl.DeviceIdType.MESH
TAU = 2.0 * math.pi

COLS = 8
GROUPS = 4
ROWS = 128
HALF = 64
TILES = 8
K2 = 512
POINTS = 512
BLOCK = 16
STEP = 4
PEERS = HALF - 1


def split_table(table):
    high = table.astype(np.float32).astype(ml_dtypes.bfloat16)
    low = (table - high.astype(np.float64)).astype(np.float32).astype(ml_dtypes.bfloat16)
    return high, low


def inner_table():
    k2 = np.arange(K2)[:, None]
    point = np.arange(1024)[None, :]
    angle = (k2 * point % 2048) * (TAU / 2048)
    cosine = np.cos(angle).reshape(K2, TILES, 128)
    sine = np.sin(angle).reshape(K2, TILES, 128)
    table = np.concatenate((cosine, sine), axis=2).transpose(1, 0, 2)
    return np.stack(split_table(table), axis=1)


def outer_table():
    place = np.arange(HALF)[:, None]
    low = np.arange(4)[None, :]
    k1 = np.stack([256 * part + 4 * place + low for part in range(2)])
    angle = (k1[..., None] * np.arange(POINTS) % POINTS) * (TAU / POINTS)
    cosine, sine = np.cos(angle), np.sin(angle)
    from_real = np.concatenate((cosine, sine), axis=3)
    from_imag = np.concatenate((-sine, cosine), axis=3)
    table = np.stack((from_real, from_imag), axis=2).reshape(2, 2 * 256, 2 * POINTS)
    return np.stack(split_table(table), axis=1)


def split(values):
    high = values.astype(jnp.bfloat16)
    return high, (values - high.astype(jnp.float32)).astype(jnp.bfloat16)


def dot(left, right):
    return jnp.dot(left, right, preferred_element_type=jnp.float32)


def swap_groups(pieces):
    lane = lax.broadcasted_iota(jnp.int32, pieces[0].shape, pieces[0].ndim - 1)
    axis = pieces[0].ndim - 1
    pieces = list(pieces)
    for bit in (4, 2, 1):
        keep = (lane // (16 * bit)) % 2 == 0
        for first in range(8):
            if first & bit:
                continue
            a, b = pieces[first], pieces[first + bit]
            pieces[first] = jnp.where(keep, a, pltpu.roll(b, 16 * bit, axis))
            pieces[first + bit] = jnp.where(keep, pltpu.roll(a, 128 - 16 * bit, axis), b)
    return pieces


def kernel(
    coeffs,
    constraint_hbm,
    alpha,
    coset,
    inner_hbm,
    outer_hbm,
    evaluations,
    quotient,
    own,
    other,
    inner,
    outer,
    x_split,
    twist,
    outgoing,
    incoming,
    part_out,
    part_in,
    edge_out,
    edge_in,
    table_sem,
    own_sem,
    pair_sem,
    send_sem,
    recv_sem,
    part_sem,
    edge_sem,
    constraint,
    small_sem,
    pair_ready,
    edge_ready,
    run_ready,
    extra,
    beyond,
    extra_sem,
):
    row = lax.axis_index("row")
    col = lax.axis_index("col")
    half = row // HALF
    place = row % HALF
    tile = place // 8
    core = place % 2
    base = half * HALF
    previous = (row + ROWS - 1) % ROWS
    following = (row + 1) % ROWS
    partner = (row + HALF) % ROWS

    barrier = pltpu.get_barrier_semaphore()

    def greet(device):
        pl.semaphore_signal(barrier, inc=1, device_id=device, device_id_type=MESH)

    def tile_of(i):
        offset = (1 + (3 + 3 * i) % 7) * (1 - i // 7)
        return (tile + offset * (1 - 2 * core) + 8) % TILES

    def load_tile(t):
        return pltpu.make_async_copy(inner_hbm.at[t], inner.at[t], table_sem.at[t])

    load_own = pltpu.make_async_copy(coeffs, own, own_sem)
    load_own.start()
    load_small = pltpu.make_async_copy(constraint_hbm, constraint, small_sem)
    load_small.start()

    @pl.loop(0, TILES)
    def _(i):
        load_tile(tile_of(i)).start()

    load_outer = pltpu.make_async_copy(outer_hbm, outer, table_sem.at[TILES])
    load_outer.start()

    first_half = half == 0
    first_row = row == 0
    last_row = row == ROWS - 1

    @pl.when(first_half)
    def _():
        greet((partner, col))

    seat = place % 8

    def in_line(i):
        return base + (tile + i) % TILES * 8 + seat

    for i in range(1, TILES):
        greet((base + 8 * tile + (place + i) % 8, col))
        greet((in_line(i), col))
    for i in range(1, GROUPS):
        greet((row, (col + i) % GROUPS))

    @pl.when((row != PEERS) & (row != ROWS - 1))
    def _():
        for i in range(GROUPS):
            greet((following, i))

    @pl.when(first_row)
    def _():
        for i in range(GROUPS):
            greet((previous, i))

    expected = 2 * (TILES - 1) + GROUPS - 1 + half
    expected = expected + jnp.where(place == 0, 0, GROUPS) + jnp.where(last_row, GROUPS, 0)

    shift = coset[0]
    k2 = lax.broadcasted_iota(jnp.int32, (1, K2), 1)
    phase = k2.astype(jnp.float32) * (shift * (TAU / 2048))
    sign = (1 - 2 * ((k2 % 2) * half)).astype(jnp.float32)
    turn = (1 - 2 * (k2 % 2)).astype(jnp.float32)
    phase_cos = jnp.cos(phase) * sign
    phase_sin = jnp.sin(phase) * sign

    wide = 128 * (TILES + 1)
    sub = lax.broadcasted_iota(jnp.int32, (8, wide), 0)
    k1 = 256 * ((half + sub // 4) % 2) + 4 * place + sub % 4
    point = 1024 * half + lax.broadcasted_iota(jnp.int32, (8, wide), 1)
    k1_f = k1.astype(jnp.float32)
    angle = ((k1 * point).astype(jnp.float32) + k1_f * shift) * (TAU / 1048576)
    cosine, sine = jnp.cos(angle), jnp.sin(angle)
    cosine_turned, sine_turned = pltpu.roll(cosine, 4, 0), pltpu.roll(sine, 4, 0)
    upper = sub < 4
    pairs = (
        (jnp.where(upper, cosine, cosine_turned), jnp.where(upper, -sine, sine_turned)),
        (jnp.where(upper, cosine_turned, cosine), jnp.where(upper, -sine_turned, sine)),
    )
    for p in range(2):
        for t in range(TILES + 1):
            twist[p, t, 0] = pairs[p][0][:, 128 * t : 128 * t + 128]
            twist[p, t, 1] = pairs[p][1][:, 128 * t : 128 * t + 128]

    def prepare(p, source):
        x = source[...]
        x = jnp.concatenate((x * phase_cos, x * phase_sin), axis=1).reshape(64, K2)
        high, low = split(x)
        x_split[p, 0] = high
        x_split[p, 1] = low

    load_own.wait()
    prepare(0, own)
    pl.semaphore_wait(barrier, expected)

    pair = pltpu.make_async_remote_copy(
        src_ref=own,
        dst_ref=other,
        send_sem=pair_sem.at[0],
        recv_sem=pair_sem.at[1],
        device_id=(partner, col),
        device_id_type=MESH,
    )

    @pl.when(half == 1)
    def _():
        pair.start()
        pl.semaphore_signal(pair_ready, inc=1, device_id=(partner, col), device_id_type=MESH)

    for i in range(1, TILES):
        pl.semaphore_signal(run_ready, inc=1, device_id=(in_line(i), col), device_id_type=MESH)

    @pl.when(last_row)
    def _():
        for i in range(GROUPS):
            pl.semaphore_signal(edge_ready, inc=1, device_id=(following, i), device_id_type=MESH)

    def send(source, target, device, sem):
        return pltpu.make_async_remote_copy(
            src_ref=source,
            dst_ref=target,
            send_sem=send_sem.at[sem],
            recv_sem=recv_sem.at[sem],
            device_id=(base + device, col),
            device_id_type=MESH,
        )

    def send_extra(part):
        return pltpu.make_async_remote_copy(
            src_ref=outgoing.at[HALF, part],
            dst_ref=extra.at[place, part],
            send_sem=extra_sem.at[0, part],
            recv_sem=extra_sem.at[1, 0],
            device_id=(base + PEERS, col),
            device_id_type=MESH,
        )

    def blocks(sem):
        where = (pl.ds(0, PEERS), 0)
        return send(outgoing.at[where], incoming.at[where], (place + 1) % HALF, sem)

    minus = jnp.where(lax.broadcasted_iota(jnp.int32, (1, 8, 128), 1) < 4, -1.0, 1.0)

    def tile_blocks(x, t, p, turned):
        ah, al = x_split[x, 0], x_split[x, 1]
        bh, bl = inner[t, 0], inner[t, 1]
        y = dot(ah, bh) + (dot(al, bh) + dot(ah, bl))
        z = y[:, :128].reshape(COLS, 8, 128)
        z = z + minus * pltpu.roll(y[:, 128:].reshape(COLS, 8, 128), 4, 1)
        z = z * twist[p, turned, 0][None] + pltpu.roll(z, 4, 1) * twist[p, turned, 1][None]
        return swap_groups([z[c] for c in range(COLS)])

    def run_tile(p, t):
        for d, block in enumerate(tile_blocks(p, t, p, t)):
            outgoing[8 * t + d, (half + p) % 2] = block

    def send_tile(p, t, first):
        part = (half + p) % 2
        for j in range(first, 8):
            device = 8 * t + (place + j) % 8
            send(outgoing.at[device, part], incoming.at[place, part], device, p).start()

    def extra_tile(p):
        part = (half + p) % 2
        for level in range(2):
            x_split[2 + p, level] = x_split[p, level] * turn.astype(jnp.bfloat16)
        outgoing[HALF, part] = tile_blocks(2 + p, 0, p, TILES)[0]

        @pl.when(place < PEERS)
        def _():
            send_extra(part).start()

    pl.semaphore_wait(run_ready, TILES - 1)

    def own_tile(i):
        t = tile_of(i)
        load_tile(t).wait()
        run_tile(0, t)
        send_tile(0, t, 0)

    pl.loop(0, TILES - 1)(own_tile)
    load_tile(tile).wait()
    run_tile(0, tile)
    send_tile(0, tile, 1)

    @pl.when(first_half)
    def _():
        extra_tile(0)
        pl.semaphore_wait(pair_ready, 1)
        pair.start()

    pair.wait_recv()
    prepare(1, other)

    @pl.loop(0, TILES - 1)
    def _(i):
        t = tile_of(i)
        run_tile(1, t)
        send_tile(1, t, 0)

    run_tile(1, tile)
    send_tile(1, tile, 1)

    @pl.when(first_half)
    def _():
        extra_tile(1)

    incoming[place] = outgoing[place]
    load_outer.wait()

    def finish(blocks_in, part):
        held = blocks_in[:, part].reshape(POINTS, 128).T
        rh, rl = split(held)
        th, tl = outer[part, 0], outer[part, 1]
        return dot(rh, th) + (dot(rl, th) + dot(rh, tl))

    @pl.when(half == 1)
    def _():
        blocks(1).wait_recv()

    @pl.when(first_half)
    def _():
        blocks(0).wait_recv()

    v = finish(incoming, 0)

    @pl.when(half == 1)
    def _():
        blocks(0).wait_recv()

    @pl.when(first_half)
    def _():
        blocks(1).wait_recv()

    v = v + finish(incoming, 1)
    real = v[:, :POINTS].reshape(COLS, BLOCK, POINTS)
    imag = v[:, POINTS:].reshape(COLS, BLOCK, POINTS)

    load_small.wait()
    a1 = alpha[0]
    a2 = a1 * a1
    a4 = a2 * a2
    a8 = a4 * a4
    weight = jnp.where(col % 2 == 1, a8, 1.0) * jnp.where(col // 2 == 1, a8 * a8, 1.0)
    first_weight = weight
    ahead_real = ahead_imag = sum_real = sum_imag = 0.0
    for c in range(COLS):
        quad = constraint[0, COLS * col + c]
        linear = constraint[1, COLS * col + c]
        vr, vi = real[c], imag[c]
        ahead_real += weight * vr
        ahead_imag += weight * vi
        sum_real += weight * (quad * (vr * vr - vi * vi) + linear * vr)
        sum_imag += weight * (quad * (2.0 * vr * vi) + linear * vi)
        weight = weight * a1

    beyond[...] = jnp.zeros((2, STEP, POINTS), jnp.float32)

    @pl.when(row == PEERS)
    def _():
        extra[place] = outgoing[HALF]
        received = pltpu.make_async_remote_copy(
            src_ref=outgoing.at[pl.ds(0, PEERS)],
            dst_ref=extra.at[pl.ds(0, PEERS)],
            send_sem=extra_sem.at[0, 0],
            recv_sem=extra_sem.at[1, 0],
            device_id=(base, col),
            device_id_type=MESH,
        )
        received.wait_recv()
        u = finish(extra, 0) + finish(extra, 1)
        edge_in[...] = jnp.zeros((GROUPS, 8, 128), jnp.float32)
        scale = first_weight
        for c in range(COLS):
            for p in range(2):
                found = u[BLOCK * c : BLOCK * c + 8, POINTS * p : POINTS * (p + 1)]
                beyond[p] += scale * found[:STEP]
            scale = scale * a1

    sum_real = jnp.concatenate((ahead_real[STEP:], beyond[0]), axis=0) - sum_real
    sum_imag = jnp.concatenate((ahead_imag[STEP:], beyond[1]), axis=0) - sum_imag
    edge = jnp.concatenate((ahead_real[:STEP], ahead_imag[:STEP]), axis=0)
    edge = jnp.where(row == 0, pltpu.roll(edge, POINTS - 1, 1), edge)
    for q in range(GROUPS):
        edge_out[q] = edge[:, 128 * q : 128 * q + 128]
        part_out[q, 0] = sum_real[:, 128 * q : 128 * q + 128]
        part_out[q, 1] = sum_imag[:, 128 * q : 128 * q + 128]

    def send_part(target):
        return pltpu.make_async_remote_copy(
            src_ref=part_out.at[target],
            dst_ref=part_in.at[col],
            send_sem=part_sem.at[0],
            recv_sem=part_sem.at[1],
            device_id=(row, target),
            device_id_type=MESH,
        )

    for i in range(1, GROUPS):
        send_part((col + i) % GROUPS).start()

    @pl.when(first_row)
    def _():
        pl.semaphore_wait(edge_ready, GROUPS)

    @pl.when(row != HALF)
    def _():
        for q in range(GROUPS):
            pltpu.make_async_remote_copy(
                src_ref=edge_out.at[q],
                dst_ref=edge_in.at[col],
                send_sem=edge_sem.at[0],
                recv_sem=edge_sem.at[1],
                device_id=(previous, q),
                device_id_type=MESH,
            ).start()

    part_in[col] = part_out[col]
    evaluations[0] = real
    evaluations[1] = imag

    point = lax.broadcasted_iota(jnp.int32, (BLOCK, 128), 0) % STEP
    theta = (shift + point.astype(jnp.float32)) * (TAU / STEP)
    van_real = jnp.cos(theta) - 1.0
    van_imag = jnp.sin(theta)
    denominator = van_real * van_real + van_imag * van_imag

    parts = pltpu.make_async_remote_copy(
        src_ref=part_out.at[pl.ds(0, GROUPS - 1)],
        dst_ref=part_in.at[pl.ds(0, GROUPS - 1)],
        send_sem=part_sem.at[0],
        recv_sem=part_sem.at[1],
        device_id=(partner, col),
        device_id_type=MESH,
    )
    edges = pltpu.make_async_remote_copy(
        src_ref=edge_out,
        dst_ref=edge_in,
        send_sem=edge_sem.at[0],
        recv_sem=edge_sem.at[1],
        device_id=(partner, col),
        device_id_type=MESH,
    )
    parts.wait_recv()

    @pl.when(row != PEERS)
    def _():
        edges.wait_recv()

    part = (part_in[0] + part_in[1]) + (part_in[2] + part_in[3])
    edge = (edge_in[0] + edge_in[1]) + (edge_in[2] + edge_in[3])
    none = jnp.zeros((BLOCK - STEP, 128), jnp.float32)
    num_real = part[0] + jnp.concatenate((none, edge[:STEP]), axis=0)
    num_imag = part[1] + jnp.concatenate((none, edge[STEP:]), axis=0)
    quotient[0] = (num_real * van_real + num_imag * van_imag) / denominator
    quotient[1] = (num_imag * van_real - num_real * van_imag) / denominator

    pair.wait_send()
    blocks(0).wait_send()
    blocks(1).wait_send()

    @pl.when(first_half & (place < PEERS))
    def _():
        send_extra(0).wait_send()
        send_extra(1).wait_send()

    parts.wait_send()

    @pl.when(row != HALF)
    def _():
        edges.wait_send()


def per_device(coeffs, constraint_coeffs, alpha, coset_shift):
    def pinned(array):
        return pltpu.with_memory_space_constraint(array, pltpu.HBM)

    tables = [pinned(jnp.asarray(table)) for table in (inner_table(), outer_table())]
    hbm = pl.BlockSpec(memory_space=pltpu.HBM)
    vmem = pl.BlockSpec(memory_space=pltpu.VMEM)
    smem = pl.BlockSpec(memory_space=pltpu.SMEM)
    f32 = jnp.float32
    bf16 = jnp.bfloat16
    return pl.pallas_call(
        kernel,
        out_shape=(
            jax.ShapeDtypeStruct((2, COLS, BLOCK, POINTS), f32),
            jax.ShapeDtypeStruct((2, BLOCK, 128), f32),
        ),
        in_specs=[hbm, hbm, smem, smem] + [hbm] * 2,
        out_specs=(vmem, vmem),
        scratch_shapes=[
            pltpu.VMEM((COLS, 4, K2), f32),
            pltpu.VMEM((COLS, 4, K2), f32),
            pltpu.VMEM((TILES, 2, K2, 256), bf16),
            pltpu.VMEM((2, 2, POINTS, 2 * POINTS), bf16),
            pltpu.VMEM((4, 2, 64, K2), bf16),
            pltpu.VMEM((2, TILES + 1, 2, 8, 128), f32),
            pltpu.VMEM((HALF + 1, 2, 8, 128), f32),
            pltpu.VMEM((HALF, 2, 8, 128), f32),
            pltpu.VMEM((GROUPS, 2, BLOCK, 128), f32),
            pltpu.VMEM((GROUPS, 2, BLOCK, 128), f32),
            pltpu.VMEM((GROUPS, 8, 128), f32),
            pltpu.VMEM((GROUPS, 8, 128), f32),
            pltpu.SemaphoreType.DMA((TILES + 1,)),
            pltpu.SemaphoreType.DMA,
            pltpu.SemaphoreType.DMA((2,)),
            pltpu.SemaphoreType.DMA((2,)),
            pltpu.SemaphoreType.DMA((2,)),
            pltpu.SemaphoreType.DMA((2,)),
            pltpu.SemaphoreType.DMA((2,)),
            pltpu.SMEM((2, GROUPS * COLS), f32),
            pltpu.SemaphoreType.DMA,
            pltpu.SemaphoreType.REGULAR,
            pltpu.SemaphoreType.REGULAR,
            pltpu.SemaphoreType.REGULAR,
            pltpu.VMEM((HALF, 2, 8, 128), f32),
            pltpu.VMEM((2, STEP, POINTS), f32),
            pltpu.SemaphoreType.DMA((2, 2)),
        ],
        compiler_params=pltpu.CompilerParams(
            collective_id=0, has_side_effects=True, vmem_limit_bytes=48 * 1024 * 1024
        ),
    )(
        pinned(coeffs),
        pinned(constraint_coeffs),
        alpha,
        coset_shift,
        *tables,
    )


def solution(mesh):
    in_specs = (P("col", "row", None), P(), P(), P())
    out_specs = (P(None, "col", "row", None), P(None, "row", "col"))
    return jax.shard_map(
        per_device, mesh=mesh, in_specs=in_specs, out_specs=out_specs, check_vma=False
    )
```
